32 devices in a mesh: col: 4 (over x, core), dp: 8 (over z, y).
Axes of the slice: x: 2, y: 2, z: 4, core: 2. Of those that a mesh axis runs over, the one named last changes fastest.
Arguments:
- layer_input: bfloat16 [1024, 8192], P('dp', 'col'), may hold values from -6 to 6
- query_cotangent: bfloat16 [1024, 4096], P('dp'), may hold values from -0.1875 to 0.1875
- key_cotangent: bfloat16 [1024, 1024], P('dp'), may hold values from -0.1875 to 0.1875
- up_cotangent: bfloat16 [1024, 14336], P('dp'), may hold values from -0.1875 to 0.1875
- query_weight: bfloat16 [4096, 8192], P('dp', 'col'), may hold values from -24 to 24
- key_weight: bfloat16 [1024, 8192], P('dp', 'col'), may hold values from -24 to 24
- up_weight: bfloat16 [14336, 8192], P('dp', 'col'), may hold values from -24 to 24
- moment_query: bfloat16 [4096, 8192], P('dp', 'col'), may hold values from -3 to 3
- moment_key: bfloat16 [1024, 8192], P('dp', 'col'), may hold values from -3 to 3
- moment_up: bfloat16 [14336, 8192], P('dp', 'col'), may hold values from -3 to 3
- second_query: bfloat16 [4096, 8192], P('dp', 'col'), may hold values from 0.25 to 4
- second_key: bfloat16 [1024, 8192], P('dp', 'col'), may hold values from 0.25 to 4
- second_up: bfloat16 [14336, 8192], P('dp', 'col'), may hold values from 0.25 to 4
Outputs:
- updated_query: bfloat16 [4096, 8192], P('dp', 'col')
- updated_key: bfloat16 [1024, 8192], P('dp', 'col')
- updated_up: bfloat16 [14336, 8192], P('dp', 'col')
- mean_query: bfloat16 [4096, 8192], P('dp', 'col')
- mean_key: bfloat16 [1024, 8192], P('dp', 'col')
- mean_up: bfloat16 [14336, 8192], P('dp', 'col')
- square_query: bfloat16 [4096, 8192], P('dp', 'col')
- square_key: bfloat16 [1024, 8192], P('dp', 'col')
- square_up: bfloat16 [14336, 8192], P('dp', 'col')
The draws below stay inside these ranges and needn't reach their ends.
All inputs are finite; a program needn't handle non-finite values.
Results may differ from the reference program's by a relative error of at most 0.001.
Values may be sent and summed in bfloat16 or wider, within the bound.
No kernel may reach another device: no remote copies, remote signals or barrier semaphores. Data moves between devices by JAX's collectives and lax.ppermute only.
A program may use at most 192 MiB of HBM per device.

```python
import math
import jax
import jax.numpy as jnp
from jax import lax

D = 8192
FF_WIN = 14336
QROWS = 4096
KROWS = 1024
TOKENS = 1024


def scaled_weight(key, rows, which):
    key = jax.random.fold_in(key, which)
    key_base = jax.random.fold_in(key, 11)
    key_cols = jax.random.fold_in(key, 12)
    key_blocks = jax.random.fold_in(key, 13)
    key_rows = jax.random.fold_in(key, 14)
    base = jnp.clip(jax.random.normal(key_base, (rows, D), jnp.float32), -4.0, 4.0)
    column_scale = jnp.exp(jax.random.uniform(key_cols, (1, D), jnp.float32, math.log(0.25), math.log(2.5)))
    block_scale = jnp.exp(jax.random.uniform(key_blocks, (32,), jnp.float32, math.log(0.5), math.log(1.5)))
    block_scale = jnp.repeat(block_scale, D // 32).reshape(1, D)
    row_scale = jnp.exp(jax.random.uniform(key_rows, (rows, 1), jnp.float32, math.log(0.4), math.log(1.6)))
    return (base * column_scale * block_scale * row_scale).astype(jnp.bfloat16)


def draw_query_weight(key, part):
    return scaled_weight(key, QROWS, 101)


def draw_key_weight(key, part):
    return scaled_weight(key, KROWS, 202)


def draw_up_weight(key, part):
    return scaled_weight(key, FF_WIN, 303)


def level_of(own_key, extent, shards, smallest, largest):
    def one(axis_at, shards_of):
        draws = jax.random.uniform(jax.random.fold_in(jax.random.fold_in(own_key, 6), axis_at), (shards_of,), jnp.float32, smallest / len(shards), largest / len(shards))
        return jnp.repeat(jnp.exp(draws), extent[axis_at] // shards_of).reshape((-1,) + (1,) * (len(extent) - axis_at - 1))

    factor_of = one(*shards[0])
    for cut in shards[1:]:
        factor_of = factor_of * one(*cut)
    return factor_of


def scatter_about(rng, extent, width, bound, cuts=(), held_as=jnp.bfloat16):
    drawn = width * jax.random.normal(rng, extent, jnp.float32)
    if cuts:
        drawn = drawn * level_of(rng, extent, cuts, -0.22, 0.18)
    return jnp.clip(drawn, -bound, bound).astype(held_as)


def setup_inputs(seed: int = 0) -> dict:
    keys = jax.random.split(jax.random.key(seed), 14)
    return {
        "layer_input": scatter_about(keys[0], (TOKENS, D), 1.0, 6.0, ((0, 8), (1, 4))),
        "query_cotangent": scatter_about(keys[1], (TOKENS, QROWS), (1.0 / TOKENS ** 0.5), 0.1875, ((0, 8),)),
        "key_cotangent": scatter_about(keys[2], (TOKENS, KROWS), (1.0 / TOKENS ** 0.5), 0.1875, ((0, 8),)),
        "up_cotangent": scatter_about(keys[3], (TOKENS, FF_WIN), (1.0 / TOKENS ** 0.5), 0.1875, ((0, 8),)),
        "query_weight": draw_query_weight(jax.random.fold_in(keys[13], 71), 0),
        "key_weight": draw_key_weight(jax.random.fold_in(keys[13], 71), 0),
        "up_weight": draw_up_weight(jax.random.fold_in(keys[13], 71), 0),
        "moment_query": scatter_about(keys[7], (QROWS, D), 0.5, 3.0, ((0, 8), (1, 4))),
        "moment_key": scatter_about(keys[8], (KROWS, D), 0.5, 3.0, ((0, 8), (1, 4))),
        "moment_up": scatter_about(keys[9], (FF_WIN, D), 0.5, 3.0, ((0, 8), (1, 4))),
        "second_query": jnp.clip(jnp.exp(math.log(4.0) - 2.7725887 * jax.random.uniform(keys[10], (QROWS, D), jnp.float32) ** level_of(keys[10], (QROWS, D), ((0, 8), (1, 4)), -0.2, 0.2)), 0.25, 4.0).astype(jnp.bfloat16),
        "second_key": jnp.clip(jnp.exp(math.log(4.0) - 2.7725887 * jax.random.uniform(keys[11], (KROWS, D), jnp.float32) ** level_of(keys[11], (KROWS, D), ((0, 8), (1, 4)), -0.2, 0.2)), 0.25, 4.0).astype(jnp.bfloat16),
        "second_up": jnp.clip(jnp.exp(math.log(4.0) - 2.7725887 * jax.random.uniform(keys[12], (FF_WIN, D), jnp.float32) ** level_of(keys[12], (FF_WIN, D), ((0, 8), (1, 4)), -0.2, 0.2)), 0.25, 4.0).astype(jnp.bfloat16),
    }


beta_one = 0.9
beta_two = 0.95
rate = 0.1
eps_adam = 1e-08
eps_norm = 1e-06

def update(cotangent, inputs, weight, moment, second):
    gradient = jnp.dot(cotangent.T, inputs, preferred_element_type=jnp.float32)
    first = beta_one * moment.astype(jnp.float32) + (1.0 - beta_one) * gradient
    square = beta_two * second.astype(jnp.float32) + (1.0 - beta_two) * gradient * gradient
    step = weight.astype(jnp.float32) - rate * first / (jnp.sqrt(square) + eps_adam)
    power = lax.optimization_barrier(jnp.mean(step * step, axis=1, keepdims=True))
    updated = (step / jnp.sqrt(power + eps_norm)).astype(jnp.bfloat16)
    return (updated, first.astype(jnp.bfloat16), square.astype(jnp.bfloat16))

def reference(layer_input, query_cotangent, key_cotangent, up_cotangent, query_weight, key_weight, up_weight, moment_query, moment_key, moment_up, second_query, second_key, second_up):
    new_query, first_query, sq_query = update(query_cotangent, layer_input, query_weight, moment_query, second_query)
    new_key, first_key, sq_key = update(key_cotangent, layer_input, key_weight, moment_key, second_key)
    new_up, first_up, sq_up = update(up_cotangent, layer_input, up_weight, moment_up, second_up)
    return (new_query, new_key, new_up, first_query, first_key, first_up, sq_query, sq_key, sq_up)
```

```python
import functools

import jax
import jax.numpy as jnp
from jax import lax
from jax.experimental import pallas as pl
from jax.experimental.pallas import tpu as pltpu
from jax.sharding import PartitionSpec as P

beta_one = 0.9
beta_two = 0.95
rate = 0.1
eps_adam = 1e-08
eps_norm = 1e-06

params = pltpu.CompilerParams(vmem_limit_bytes=56 * 1024 * 1024)


def row_block(rows, largest=256):
    for block in range(largest, 0, -128):
        if rows % block == 0:
            return block
    return rows


def row_chunks(rows, count):
    block = row_block(rows)
    blocks = rows // block
    count = min(count, blocks)
    edges = [block * (-(-blocks * at // count)) for at in range(count + 1)]
    return list(zip(edges, edges[1:]))


def strip_of(width, largest=512):
    for strip in range(min(largest, width), 0, -128):
        if width % strip == 0:
            return strip
    return width


def pack_kernel(plan, groups, at_ref, *refs):
    inputs, outputs = refs[: -len(plan)], refs[-len(plan) :]
    for (source, rows, low, high), out_ref in zip(plan, outputs):
        for group in range(groups):
            out_ref[group] = inputs[source][:, group * rows + low : group * rows + high]


def pack(cotangents, plan, groups, part, place):
    return pl.pallas_call(
        functools.partial(pack_kernel, plan, groups),
        grid_spec=pltpu.PrefetchScalarGridSpec(
            num_scalar_prefetch=1,
            grid=(1,),
            in_specs=[
                pl.BlockSpec((part, array.shape[1]), lambda i, at: (at[0], 0))
                for array in cotangents
            ],
            out_specs=[
                pl.BlockSpec((groups, part, high - low), lambda i, at: (0, 0, 0))
                for _, _, low, high in plan
            ],
        ),
        out_shape=[
            jax.ShapeDtypeStruct((groups, part, high - low), jnp.bfloat16)
            for _, _, low, high in plan
        ],
        compiler_params=params,
        cost_estimate=pl.CostEstimate(
            flops=0,
            bytes_accessed=sum(4 * part * array.shape[1] for array in cotangents),
            transcendentals=0,
        ),
        name="pack",
    )(place, *cotangents)


def adam_kernel(strip, c_ref, x_ref, w_ref, m_ref, v_ref, *refs):
    step_ref, power_ref, first_ref, square_ref = refs[-4:]
    cols, groups, part, rows = c_ref.shape
    width = x_ref.shape[1]
    lhs = jnp.concatenate(
        [c_ref[at, group] for group in range(groups) for at in range(cols)], axis=0
    ).T
    power = jnp.zeros((rows, 128), jnp.float32)
    for start in range(0, width, strip):
        at = slice(start, start + strip)
        grad = jnp.dot(lhs, x_ref[:, at], preferred_element_type=jnp.float32)
        first = beta_one * m_ref[:, at].astype(jnp.float32) + (1.0 - beta_one) * grad
        square = beta_two * v_ref[:, at].astype(jnp.float32) + (1.0 - beta_two) * grad * grad
        step = w_ref[:, at].astype(jnp.float32) - rate * first / (jnp.sqrt(square) + eps_adam)
        first_ref[:, at] = first.astype(jnp.bfloat16)
        square_ref[:, at] = square.astype(jnp.bfloat16)
        step_ref[:, at] = step
        for lane in range(0, strip, 128):
            piece = step[:, lane : lane + 128]
            power += piece * piece
    power_ref[...] = jnp.sum(power.T, axis=0, keepdims=True)


def adam_pass(cotangent, inputs, state, low, high, made):
    cols, groups, part, rows = cotangent.shape
    tokens, width = inputs.shape
    total = state[0].shape[0]
    block = row_block(total)
    shift = low // block
    tile = pl.BlockSpec((block, width), lambda i: (i + shift, 0))
    return pl.pallas_call(
        functools.partial(adam_kernel, strip_of(width)),
        grid=(rows // block,),
        in_specs=[
            pl.BlockSpec((cols, groups, part, block), lambda i: (0, 0, 0, i)),
            pl.BlockSpec((tokens, width), lambda i: (0, 0), pipeline_mode=pl.Buffered(1)),
            tile,
            tile,
            tile,
        ]
        + [pl.BlockSpec(memory_space=pl.ANY)] * len(made),
        out_specs=[
            pl.BlockSpec((block, width), lambda i: (i, 0)),
            pl.BlockSpec((1, block), lambda i: (0, i)),
            tile,
            tile,
        ],
        out_shape=[
            jax.ShapeDtypeStruct((rows, width), jnp.float32),
            jax.ShapeDtypeStruct((1, rows), jnp.float32),
            jax.ShapeDtypeStruct((total, width), jnp.bfloat16),
            jax.ShapeDtypeStruct((total, width), jnp.bfloat16),
        ],
        input_output_aliases={5 + at: 2 + at for at in range(len(made))},
        compiler_params=params,
        cost_estimate=pl.CostEstimate(
            flops=2 * tokens * rows * width,
            bytes_accessed=14 * rows * width + 2 * tokens * (rows + width),
            transcendentals=0,
        ),
        name="adam",
    )(cotangent, inputs, *state, *made)


def finish_kernel(count, whole_width, step_ref, *refs):
    out_ref = refs[-1]
    power = refs[0][...]
    for other in refs[1:count]:
        power = power + other[...]
    scale = 1.0 / jnp.sqrt(power / whole_width + eps_norm)
    scale = jnp.broadcast_to(scale, (128, scale.shape[1])).T
    for lane in range(0, step_ref.shape[1], 128):
        at = slice(lane, lane + 128)
        out_ref[:, at] = (step_ref[:, at] * scale).astype(jnp.bfloat16)


def finish_rows(step, powers, whole_width, total, low, made):
    rows, width = step.shape
    block = row_block(total)
    shift = low // block
    return pl.pallas_call(
        functools.partial(finish_kernel, len(powers), whole_width),
        grid=(rows // block,),
        in_specs=[pl.BlockSpec((block, width), lambda i: (i, 0))]
        + [pl.BlockSpec((1, block), lambda i: (0, i))] * len(powers)
        + [pl.BlockSpec(memory_space=pl.ANY)] * len(made),
        out_specs=[pl.BlockSpec((block, width), lambda i: (i + shift, 0))],
        out_shape=[jax.ShapeDtypeStruct((total, width), jnp.bfloat16)],
        input_output_aliases={1 + len(powers) + at: at for at in range(len(made))},
        compiler_params=params,
        cost_estimate=pl.CostEstimate(
            flops=rows * width, bytes_accessed=6 * rows * width, transcendentals=0
        ),
        name="finish",
    )(step, *powers, *made)


def from_others(array, axis):
    size = lax.axis_size(axis)
    return [
        lax.ppermute(array, axis, [(at, (at + turn) % size) for at in range(size)])
        for turn in range(1, size)
    ]


def per_device(
    layer_input,
    query_cotangent,
    key_cotangent,
    up_cotangent,
    query_weight,
    key_weight,
    up_weight,
    moment_query,
    moment_key,
    moment_up,
    second_query,
    second_key,
    second_up,
):
    groups = lax.axis_size("dp")
    cols = lax.axis_size("col")
    part = layer_input.shape[0] // cols
    whole_width = layer_input.shape[1] * cols
    states = (
        (query_weight, moment_query, second_query),
        (key_weight, moment_key, second_key),
        (up_weight, moment_up, second_up),
    )
    plan = [
        (at, state[0].shape[0], low, high)
        for at, state, count in zip(range(3), states, (1, 1, 2))
        for low, high in row_chunks(state[0].shape[0], count)
    ]
    place = lax.axis_index("col").astype(jnp.int32).reshape(1)
    packed = pack((query_cotangent, key_cotangent, up_cotangent), plan, groups, part, place)
    gathered = lax.all_gather(layer_input, "dp", axis=0, tiled=True)
    owned = [
        lax.all_to_all(array, "dp", split_axis=0, concat_axis=0, tiled=True) for array in packed
    ]
    every = [lax.all_gather(array, "col", axis=0) for array in owned]
    moments = [[], [], []]
    updated = [[], [], []]
    for (at, total, low, high), cotangent in zip(plan, every):
        step, power, *moments[at] = adam_pass(
            cotangent, gathered, states[at], low, high, moments[at]
        )
        powers = [power, *from_others(power, "col")]
        updated[at] = finish_rows(step, powers, whole_width, total, low, updated[at])
    return (
        *(made[0] for made in updated),
        *(made[0] for made in moments),
        *(made[1] for made in moments),
    )


def solution(mesh):
    tokens_split = P("dp", None)
    split = P("dp", "col")
    return jax.shard_map(
        per_device,
        mesh=mesh,
        in_specs=(split, *(tokens_split,) * 3, *(split,) * 9),
        out_specs=(split,) * 9,
        check_vma=False,
    )
```

```python
import functools

import jax
import jax.numpy as jnp
from jax import lax
from jax.experimental import pallas as pl
from jax.experimental.pallas import tpu as pltpu
from jax.sharding import PartitionSpec as P

beta_one = 0.9
beta_two = 0.95
rate = 0.1
eps_adam = 1e-08
eps_norm = 1e-06


def with_vmem(mebibytes):
    return pltpu.CompilerParams(vmem_limit_bytes=mebibytes * 1024 * 1024)


def row_block(rows, largest=256):
    for block in range(largest, 0, -128):
        if rows % block == 0:
            return block
    return rows


def column_chunk(width, count):
    while width % (count * 128):
        count -= 1
    return width // count


def strip_of(width, largest=512):
    for strip in range(min(largest, width), 0, -128):
        if width % strip == 0:
            return strip
    return width


def pack_kernel(groups, *refs):
    out_ref = refs[-1]
    low = 0
    for ref in refs[1:-1]:
        rows = ref.shape[1] // groups
        for group in range(groups):
            out_ref[group, :, low : low + rows] = ref[:, group * rows : (group + 1) * rows]
        low += rows


def pack(cotangents, groups, part, place):
    rows = sum(array.shape[1] for array in cotangents) // groups
    return pl.pallas_call(
        functools.partial(pack_kernel, groups),
        grid_spec=pltpu.PrefetchScalarGridSpec(
            num_scalar_prefetch=1,
            grid=(1,),
            in_specs=[
                pl.BlockSpec((part, array.shape[1]), lambda i, at: (at[0], 0))
                for array in cotangents
            ],
            out_specs=pl.BlockSpec((groups, part, rows), lambda i, at: (0, 0, 0)),
        ),
        out_shape=jax.ShapeDtypeStruct((groups, part, rows), jnp.bfloat16),
        compiler_params=with_vmem(12),
        cost_estimate=pl.CostEstimate(
            flops=0, bytes_accessed=4 * groups * part * rows, transcendentals=0
        ),
        name="pack",
    )(place, *cotangents)


def unpack_kernel(count, at_ref, *refs):
    pieces, outputs, order = refs[:count], refs[count:-1], refs[-1]
    groups, part, _ = pieces[0].shape
    for turn, piece in enumerate(pieces):
        for group in range(groups):
            order[group * count + (at_ref[0] ^ turn)] = piece[group]
    low = 0
    for out_ref in outputs:
        rows = out_ref.shape[0]
        for start in range(0, rows, 128):
            high = min(start + 128, rows)
            tokens = order[:, :, low + start : low + high].reshape(-1, high - start)
            out_ref[start:high] = tokens.T
        low += rows


def unpack(pieces, row_counts, place):
    groups, part, rows = pieces[0].shape
    tokens = groups * part * len(pieces)
    vmem = pl.BlockSpec(memory_space=pltpu.VMEM)
    return pl.pallas_call(
        functools.partial(unpack_kernel, len(pieces)),
        in_specs=[pl.BlockSpec(memory_space=pltpu.SMEM)] + [vmem] * len(pieces),
        out_specs=[vmem] * len(row_counts),
        out_shape=[jax.ShapeDtypeStruct((count, tokens), jnp.bfloat16) for count in row_counts],
        scratch_shapes=[pltpu.VMEM((groups * len(pieces), part, rows), jnp.bfloat16)],
        compiler_params=with_vmem(28),
        cost_estimate=pl.CostEstimate(
            flops=0, bytes_accessed=4 * tokens * rows, transcendentals=0
        ),
        name="unpack",
    )(place, *pieces)


def adam_kernel(strip, c_ref, x_ref, w_ref, m_ref, v_ref, *refs):
    power_ref, step_ref, first_ref, square_ref = refs[-4:]
    rows = c_ref.shape[0]
    width = x_ref.shape[1]
    lhs = c_ref[...]
    power = jnp.zeros((rows, 128), jnp.float32)
    for start in range(0, width, strip):
        at = slice(start, start + strip)
        grad = jnp.dot(lhs, x_ref[:, at], preferred_element_type=jnp.float32)
        first = beta_one * m_ref[:, at].astype(jnp.float32) + (1.0 - beta_one) * grad
        square = beta_two * v_ref[:, at].astype(jnp.float32) + (1.0 - beta_two) * grad * grad
        root = square * lax.rsqrt(square) + eps_adam
        inverse = pl.reciprocal(root, approx=True)
        inverse = inverse * (2.0 - root * inverse)
        step = w_ref[:, at].astype(jnp.float32) - rate * first * inverse
        first_ref[:, at] = first.astype(jnp.bfloat16)
        square_ref[:, at] = square.astype(jnp.bfloat16)
        step_ref[:, at] = step
        for lane in range(0, strip, 128):
            piece = step[:, lane : lane + 128]
            power += piece * piece
    power = jnp.sum(power.T, axis=0, keepdims=True)
    if len(refs) > 4:
        power += refs[0][...]
    power_ref[...] = power


def adam_pass(cotangent, inputs, state, chunk, made):
    rows, tokens = cotangent.shape
    width = inputs.shape[1]
    whole = state[0].shape[1]
    block = row_block(rows)
    tile = pl.BlockSpec((block, width), lambda i: (i, chunk))
    power = pl.BlockSpec((1, block), lambda i: (0, i))
    return pl.pallas_call(
        functools.partial(adam_kernel, strip_of(width)),
        grid=(rows // block,),
        in_specs=[
            pl.BlockSpec((block, tokens), lambda i: (i, 0)),
            pl.BlockSpec((tokens, width), lambda i: (0, 0), pipeline_mode=pl.Buffered(1)),
            tile,
            tile,
            tile,
        ]
        + ([power] + [pl.BlockSpec(memory_space=pl.ANY)] * 3 if made else []),
        out_specs=[power, tile, tile, tile],
        out_shape=[
            jax.ShapeDtypeStruct((1, rows), jnp.float32),
            jax.ShapeDtypeStruct((rows, whole), jnp.float32),
            jax.ShapeDtypeStruct((rows, whole), jnp.bfloat16),
            jax.ShapeDtypeStruct((rows, whole), jnp.bfloat16),
        ],
        input_output_aliases={5 + at: at for at in range(len(made))},
        compiler_params=with_vmem(48),
        cost_estimate=pl.CostEstimate(
            flops=2 * tokens * rows * width,
            bytes_accessed=14 * rows * width + 2 * tokens * (rows + width),
            transcendentals=0,
        ),
        name="adam",
    )(cotangent, inputs, *state, *made)


def finish_kernel(count, whole_width, step_ref, *refs):
    out_ref = refs[-1]
    power = refs[0][...]
    for other in refs[1:count]:
        power = power + other[...]
    scale = 1.0 / jnp.sqrt(power / whole_width + eps_norm)
    scale = jnp.broadcast_to(scale, (128, scale.shape[1])).T
    for lane in range(0, step_ref.shape[1], 128):
        at = slice(lane, lane + 128)
        out_ref[:, at] = (step_ref[:, at] * scale).astype(jnp.bfloat16)


def finish_rows(step, powers, whole_width):
    rows, width = step.shape
    block = row_block(rows)
    tile = pl.BlockSpec((block, width), lambda i: (i, 0))
    return pl.pallas_call(
        functools.partial(finish_kernel, len(powers), whole_width),
        grid=(rows // block,),
        in_specs=[tile] + [pl.BlockSpec((1, block), lambda i: (0, i))] * len(powers),
        out_specs=tile,
        out_shape=jax.ShapeDtypeStruct((rows, width), jnp.bfloat16),
        compiler_params=with_vmem(24),
        cost_estimate=pl.CostEstimate(
            flops=rows * width, bytes_accessed=6 * rows * width, transcendentals=0
        ),
        name="finish",
    )(step, *powers)


def from_others(array, axis):
    size = lax.axis_size(axis)
    bit = size // 2
    got = {0: array}
    while bit:
        for turn in list(got):
            got[turn ^ bit] = lax.ppermute(got[turn], axis, [(at, at ^ bit) for at in range(size)])
        bit //= 2
    return [got[turn] for turn in range(size)]


def per_device(
    layer_input,
    query_cotangent,
    key_cotangent,
    up_cotangent,
    query_weight,
    key_weight,
    up_weight,
    moment_query,
    moment_key,
    moment_up,
    second_query,
    second_key,
    second_up,
):
    groups = lax.axis_size("dp")
    cols = lax.axis_size("col")
    part = layer_input.shape[0] // cols
    whole_width = layer_input.shape[1] * cols
    states = (
        (query_weight, moment_query, second_query),
        (key_weight, moment_key, second_key),
        (up_weight, moment_up, second_up),
    )
    counts = [state[0].shape[0] for state in states]
    place = lax.axis_index("col").astype(jnp.int32).reshape(1)
    packed = pack((query_cotangent, key_cotangent, up_cotangent), groups, part, place)
    owned = lax.all_to_all(packed, "dp", split_axis=0, concat_axis=0, tiled=True)
    layer_input, owned = lax.optimization_barrier((layer_input, owned))
    chunk = column_chunk(layer_input.shape[1], 2)
    gathered = [
        lax.all_gather(layer_input[:, low : low + chunk], "dp", axis=0, tiled=True)
        for low in range(0, layer_input.shape[1], chunk)
    ]
    every = unpack(from_others(owned, "col"), counts, place)
    made = [(), (), ()]
    for at, inputs in enumerate(gathered):
        for which in (2, 0, 1):
            made[which] = adam_pass(every[which], inputs, states[which], at, made[which])
    updated = [None] * 3
    for which in (2, 0, 1):
        updated[which] = finish_rows(
            made[which][1], from_others(made[which][0], "col"), whole_width
        )
    return (*updated, *(done[2] for done in made), *(done[3] for done in made))


def solution(mesh):
    tokens_split = P("dp", None)
    split = P("dp", "col")
    return jax.shard_map(
        per_device,
        mesh=mesh,
        in_specs=(split, *(tokens_split,) * 3, *(split,) * 9),
        out_specs=(split,) * 9,
        check_vma=False,
    )
```

```python
import functools

import jax
import jax.numpy as jnp
from jax import lax
from jax.experimental import pallas as pl
from jax.experimental.pallas import tpu as pltpu
from jax.sharding import PartitionSpec as P

beta_one = 0.9
beta_two = 0.95
rate = 0.1
eps_adam = 1e-08
eps_norm = 1e-06


def with_vmem(mebibytes):
    return pltpu.CompilerParams(vmem_limit_bytes=mebibytes * 1024 * 1024)


def row_block(rows, largest=256):
    for block in range(largest, 0, -128):
        if rows % block == 0:
            return block
    return rows


def chunk_plan(totals):
    first = [(which, 0, total) for which, total in enumerate(totals[:-1])]
    up = len(totals) - 1
    block = row_block(totals[up])
    blocks = totals[up] // block
    edges = sorted({0, block * (-(-blocks // 2)), totals[up]})
    return [first] + [[(up, low, high)] for low, high in zip(edges, edges[1:])]


def column_chunk(width, count):
    while width % (count * 128):
        count -= 1
    return width // count


def strip_of(width, largest=512):
    for strip in range(min(largest, width), 0, -128):
        if width % strip == 0:
            return strip
    return width


def ring_order(groups):
    return [*range(0, groups, 2), *range(groups - 1 - groups % 2, 0, -2)]


def ring_place(at, groups):
    return jnp.where(at % 2 == 0, at // 2, groups - 1 - at // 2)


def pack_kernel(plan, groups, at_ref, *refs):
    count = len(plan) * groups
    inputs, outputs, whole = refs[: -count - 1], refs[-count - 1 : -1], refs[-1]
    edges = [0]
    for ref in inputs:
        rows = ref.shape[1] // groups
        low = edges[-1]
        for group in range(groups):
            whole[group, :, low : low + rows] = ref[:, group * rows : (group + 1) * rows]
        edges.append(low + rows)
    for chunk, pieces in enumerate(plan):
        for turn in range(groups):
            to = (at_ref[1] + turn) % groups
            out_ref = outputs[chunk * groups + turn]
            start = 0
            for which, low, high in pieces:
                out_ref[:, start : start + high - low] = whole[
                    to, :, edges[which] + low : edges[which] + high
                ]
                start += high - low


def pack(cotangents, plan, groups, part, place):
    rows = sum(array.shape[1] for array in cotangents) // groups
    outs = [
        jax.ShapeDtypeStruct((part, sum(high - low for _, low, high in pieces)), jnp.bfloat16)
        for pieces in plan
        for _ in range(groups)
    ]
    return pl.pallas_call(
        functools.partial(pack_kernel, plan, groups),
        grid_spec=pltpu.PrefetchScalarGridSpec(
            num_scalar_prefetch=1,
            grid=(1,),
            in_specs=[
                pl.BlockSpec((part, array.shape[1]), lambda i, at: (at[0], 0))
                for array in cotangents
            ],
            out_specs=[pl.BlockSpec(out.shape, lambda i, at: (0, 0)) for out in outs],
            scratch_shapes=[pltpu.VMEM((groups, part, rows), jnp.bfloat16)],
        ),
        out_shape=outs,
        compiler_params=with_vmem(56),
        cost_estimate=pl.CostEstimate(
            flops=0, bytes_accessed=4 * groups * part * rows, transcendentals=0
        ),
        name="pack",
    )(place, *cotangents)


def bundle_kernel(at_ref, *refs):
    pieces, out_ref = refs[:-1], refs[-1]
    groups = len(pieces)
    here = at_ref[1]
    for turn, piece in enumerate(pieces):
        source = (here + groups - turn) % groups
        slot = ring_place(source, groups) - ring_place(here, groups) + groups
        out_ref[slot % groups] = piece[...]


def bundle(pieces, place):
    part, rows = pieces[0].shape
    vmem = pl.BlockSpec(memory_space=pltpu.VMEM)
    return pl.pallas_call(
        bundle_kernel,
        in_specs=[pl.BlockSpec(memory_space=pltpu.SMEM)] + [vmem] * len(pieces),
        out_specs=vmem,
        out_shape=jax.ShapeDtypeStruct((len(pieces), part, rows), jnp.bfloat16),
        compiler_params=with_vmem(8),
        cost_estimate=pl.CostEstimate(
            flops=0, bytes_accessed=4 * len(pieces) * part * rows, transcendentals=0
        ),
        name="bundle",
    )(place, *pieces)


def collect_kernel(*refs):
    pieces, out_ref = refs[:-1], refs[-1]
    low = 0
    for piece in pieces:
        out_ref[low : low + piece.shape[0]] = piece[...]
        low += piece.shape[0]


def collect(pieces):
    tokens = sum(piece.shape[0] for piece in pieces)
    width = pieces[0].shape[1]
    vmem = pl.BlockSpec(memory_space=pltpu.VMEM)
    block = column_chunk(width, 4)
    return pl.pallas_call(
        collect_kernel,
        grid=(width // block,),
        in_specs=[pl.BlockSpec((piece.shape[0], block), lambda i: (0, i)) for piece in pieces],
        out_specs=pl.BlockSpec((tokens, block), lambda i: (0, i)),
        out_shape=jax.ShapeDtypeStruct((tokens, width), jnp.bfloat16),
        compiler_params=with_vmem(48),
        cost_estimate=pl.CostEstimate(
            flops=0, bytes_accessed=4 * tokens * width, transcendentals=0
        ),
        name="collect",
    )(*pieces)


def gather_ring(array, axis):
    groups = lax.axis_size(axis)
    order = ring_order(groups)
    onward = list(zip(order, order[1:] + order[:1]))
    back = [(to, at) for at, to in onward]
    behind, ahead = [array], [array]
    for _ in range((groups - 1) // 2):
        behind.append(lax.ppermute(behind[-1], axis, onward))
        ahead.append(lax.ppermute(ahead[-1], axis, back))
    middle = []
    if groups % 2 == 0:
        half = array.shape[0] // 2
        middle.append(lax.ppermute(behind[-1][:half], axis, onward))
        middle.append(lax.ppermute(ahead[-1][half:], axis, back))
    return collect([array, *ahead[1:], *middle, *behind[:0:-1]])


def unpack_kernel(count, at_ref, *refs):
    pieces, outputs, order = refs[:count], refs[count:-1], refs[-1]
    groups, part, _ = pieces[0].shape
    for turn, piece in enumerate(pieces):
        for group in range(groups):
            order[group * count + (at_ref[0] ^ turn)] = piece[group]
    low = 0
    for out_ref in outputs:
        rows = out_ref.shape[0]
        for start in range(0, rows, 128):
            high = min(start + 128, rows)
            tokens = order[:, :, low + start : low + high].reshape(-1, high - start)
            out_ref[start:high] = tokens.T
        low += rows


def unpack(pieces, row_counts, place):
    groups, part, rows = pieces[0].shape
    tokens = groups * part * len(pieces)
    vmem = pl.BlockSpec(memory_space=pltpu.VMEM)
    return pl.pallas_call(
        functools.partial(unpack_kernel, len(pieces)),
        in_specs=[pl.BlockSpec(memory_space=pltpu.SMEM)] + [vmem] * len(pieces),
        out_specs=[vmem] * len(row_counts),
        out_shape=[jax.ShapeDtypeStruct((count, tokens), jnp.bfloat16) for count in row_counts],
        scratch_shapes=[pltpu.VMEM((groups * len(pieces), part, rows), jnp.bfloat16)],
        compiler_params=with_vmem(28),
        cost_estimate=pl.CostEstimate(
            flops=0, bytes_accessed=4 * tokens * rows, transcendentals=0
        ),
        name="unpack",
    )(place, *pieces)


def adam_kernel(strip, c_ref, x_ref, w_ref, m_ref, v_ref, *refs):
    power_ref, step_ref, first_ref, square_ref = refs[-4:]
    rows = c_ref.shape[0]
    width = x_ref.shape[1]
    lhs = c_ref[...]
    power = jnp.zeros((rows, 128), jnp.float32)
    for start in range(0, width, strip):
        at = slice(start, start + strip)
        grad = jnp.dot(lhs, x_ref[:, at], preferred_element_type=jnp.float32)
        first = beta_one * m_ref[:, at].astype(jnp.float32) + (1.0 - beta_one) * grad
        square = beta_two * v_ref[:, at].astype(jnp.float32) + (1.0 - beta_two) * grad * grad
        root = square * lax.rsqrt(square) + eps_adam
        inverse = pl.reciprocal(root, approx=True)
        inverse = inverse * (2.0 - root * inverse)
        step = w_ref[:, at].astype(jnp.float32) - rate * first * inverse
        first_ref[:, at] = first.astype(jnp.bfloat16)
        square_ref[:, at] = square.astype(jnp.bfloat16)
        step_ref[:, at] = step
        for lane in range(0, strip, 128):
            piece = step[:, lane : lane + 128]
            power += piece * piece
    power_ref[...] = jnp.sum(power.T, axis=0, keepdims=True)


def adam_pass(cotangent, inputs, state, low, made):
    rows, tokens = cotangent.shape
    total, width = state[0].shape
    block = row_block(total)
    shift = low // block
    tile = pl.BlockSpec((block, width), lambda i: (i + shift, 0))
    return pl.pallas_call(
        functools.partial(adam_kernel, strip_of(width)),
        grid=(rows // block,),
        in_specs=[
            pl.BlockSpec((block, tokens), lambda i: (i, 0)),
            pl.BlockSpec((tokens, width), lambda i: (0, 0), pipeline_mode=pl.Buffered(1)),
            tile,
            tile,
            tile,
        ]
        + [pl.BlockSpec(memory_space=pl.ANY)] * len(made),
        out_specs=[
            pl.BlockSpec((1, block), lambda i: (0, i)),
            pl.BlockSpec((block, width), lambda i: (i, 0)),
            tile,
            tile,
        ],
        out_shape=[
            jax.ShapeDtypeStruct((1, rows), jnp.float32),
            jax.ShapeDtypeStruct((rows, width), jnp.float32),
            jax.ShapeDtypeStruct((total, width), jnp.bfloat16),
            jax.ShapeDtypeStruct((total, width), jnp.bfloat16),
        ],
        input_output_aliases={5 + at: 2 + at for at in range(len(made))},
        compiler_params=with_vmem(48),
        cost_estimate=pl.CostEstimate(
            flops=2 * tokens * rows * width,
            bytes_accessed=14 * rows * width + 2 * tokens * (rows + width),
            transcendentals=0,
        ),
        name="adam",
    )(cotangent, inputs, *state, *made)


def finish_kernel(count, whole_width, step_ref, *refs):
    out_ref = refs[-1]
    power = refs[0][...]
    for other in refs[1:count]:
        power = power + other[...]
    scale = 1.0 / jnp.sqrt(power / whole_width + eps_norm)
    scale = jnp.broadcast_to(scale, (128, scale.shape[1])).T
    for lane in range(0, step_ref.shape[1], 128):
        at = slice(lane, lane + 128)
        out_ref[:, at] = (step_ref[:, at] * scale).astype(jnp.bfloat16)


def finish_rows(step, powers, whole_width, total, low, made):
    rows, width = step.shape
    block = row_block(total)
    shift = low // block
    return pl.pallas_call(
        functools.partial(finish_kernel, len(powers), whole_width),
        grid=(rows // block,),
        in_specs=[pl.BlockSpec((block, width), lambda i: (i, 0))]
        + [pl.BlockSpec((1, block), lambda i: (0, i))] * len(powers)
        + [pl.BlockSpec(memory_space=pl.ANY)] * len(made),
        out_specs=[pl.BlockSpec((block, width), lambda i: (i + shift, 0))],
        out_shape=[jax.ShapeDtypeStruct((total, width), jnp.bfloat16)],
        input_output_aliases={1 + len(powers) + at: at for at in range(len(made))},
        compiler_params=with_vmem(24),
        cost_estimate=pl.CostEstimate(
            flops=rows * width, bytes_accessed=6 * rows * width, transcendentals=0
        ),
        name="finish",
    )(step, *powers, *made)


def from_others(array, axis):
    size = lax.axis_size(axis)
    bit = size // 2
    got = {0: array}
    while bit:
        for turn in list(got):
            got[turn ^ bit] = lax.ppermute(got[turn], axis, [(at, at ^ bit) for at in range(size)])
        bit //= 2
    return [got[turn] for turn in range(size)]


def exchange(arrays, axis):
    size = lax.axis_size(axis)
    return [
        lax.ppermute(array, axis, [(at, (at + turn) % size) for at in range(size)])
        for turn, array in enumerate(arrays, 1)
    ]


def per_device(
    layer_input,
    query_cotangent,
    key_cotangent,
    up_cotangent,
    query_weight,
    key_weight,
    up_weight,
    moment_query,
    moment_key,
    moment_up,
    second_query,
    second_key,
    second_up,
):
    groups = lax.axis_size("dp")
    cols = lax.axis_size("col")
    part = layer_input.shape[0] // cols
    whole_width = layer_input.shape[1] * cols
    states = (
        (query_weight, moment_query, second_query),
        (key_weight, moment_key, second_key),
        (up_weight, moment_up, second_up),
    )
    plan = chunk_plan([state[0].shape[0] for state in states])
    place = jnp.stack([lax.axis_index("col"), lax.axis_index("dp")]).astype(jnp.int32)
    packed = pack((query_cotangent, key_cotangent, up_cotangent), plan, groups, part, place)
    gathered = gather_ring(layer_input, "dp")
    moments = [[], [], []]
    updated = [[], [], []]
    for chunk, pieces in enumerate(plan):
        sent = packed[chunk * groups : (chunk + 1) * groups]
        owned = bundle([sent[0], *exchange(sent[1:], "dp")], place)
        every = unpack(from_others(owned, "col"), [high - low for _, low, high in pieces], place)
        for (which, low, high), cotangent in zip(pieces, every):
            power, step, *moments[which] = adam_pass(
                cotangent, gathered, states[which], low, moments[which]
            )
            powers = from_others(power, "col")
            updated[which] = finish_rows(
                step, powers, whole_width, states[which][0].shape[0], low, updated[which]
            )
    return (
        *(made[0] for made in updated),
        *(made[0] for made in moments),
        *(made[1] for made in moments),
    )


def solution(mesh):
    tokens_split = P("dp", None)
    split = P("dp", "col")
    return jax.shard_map(
        per_device,
        mesh=mesh,
        in_specs=(split, *(tokens_split,) * 3, *(split,) * 9),
        out_specs=(split,) * 9,
        check_vma=False,
    )
```

```python
import functools

import jax
import jax.numpy as jnp
from jax import lax
from jax.experimental import pallas as pl
from jax.experimental.pallas import tpu as pltpu
from jax.sharding import PartitionSpec as P

beta_one = 0.9
beta_two = 0.95
rate = 0.1
eps_adam = 1e-08
eps_norm = 1e-06


def with_vmem(mebibytes):
    return pltpu.CompilerParams(vmem_limit_bytes=mebibytes * 1024 * 1024)


def row_block(rows, largest=256):
    for block in range(largest, 0, -128):
        if rows % block == 0:
            return block
    return rows


def chunk_plan(totals):
    first = [(which, 0, total) for which, total in enumerate(totals[:-1])]
    up = len(totals) - 1
    block = row_block(totals[up])
    blocks = max(0, (sum(totals) // 2 - sum(totals[:-1])) // block)
    if blocks:
        first.append((up, 0, blocks * block))
    return [first, [(up, blocks * block, totals[up])]]


def column_chunk(width, count):
    while width % (count * 128):
        count -= 1
    return width // count


def strip_of(width, largest=512):
    for strip in range(min(largest, width), 0, -128):
        if width % strip == 0:
            return strip
    return width


def ring_order(groups):
    return [*range(0, groups, 2), *range(groups - 1 - groups % 2, 0, -2)]


def ring_place(at, groups):
    return jnp.where(at % 2 == 0, at // 2, groups - 1 - at // 2)


def pack_kernel(plan, groups, at_ref, *refs):
    inputs, outputs = refs[: -len(plan)], refs[-len(plan) :]
    for pieces, out_ref in zip(plan, outputs):
        start = 0
        for which, low, high in pieces:
            ref = inputs[which]
            rows = ref.shape[1] // groups
            for group in range(groups):
                out_ref[group, :, start : start + high - low] = ref[
                    :, group * rows + low : group * rows + high
                ]
            start += high - low


def pack(cotangents, plan, groups, part, place):
    outs = [
        jax.ShapeDtypeStruct(
            (groups, part, sum(high - low for _, low, high in pieces)), jnp.bfloat16
        )
        for pieces in plan
    ]
    return pl.pallas_call(
        functools.partial(pack_kernel, plan, groups),
        grid_spec=pltpu.PrefetchScalarGridSpec(
            num_scalar_prefetch=1,
            grid=(1,),
            in_specs=[
                pl.BlockSpec((part, array.shape[1]), lambda i, at: (at[0], 0))
                for array in cotangents
            ],
            out_specs=[pl.BlockSpec(out.shape, lambda i, at: (0, 0, 0)) for out in outs],
        ),
        out_shape=outs,
        compiler_params=with_vmem(56),
        cost_estimate=pl.CostEstimate(
            flops=0,
            bytes_accessed=4 * part * sum(array.shape[1] for array in cotangents),
            transcendentals=0,
        ),
        name="pack",
    )(place, *cotangents)


def collect_kernel(*refs):
    pieces, out_ref = refs[:-1], refs[-1]
    low = 0
    for piece in pieces:
        out_ref[low : low + piece.shape[0]] = piece[...]
        low += piece.shape[0]


def collect(pieces):
    tokens = sum(piece.shape[0] for piece in pieces)
    width = pieces[0].shape[1]
    vmem = pl.BlockSpec(memory_space=pltpu.VMEM)
    block = column_chunk(width, 4)
    return pl.pallas_call(
        collect_kernel,
        grid=(width // block,),
        in_specs=[pl.BlockSpec((piece.shape[0], block), lambda i: (0, i)) for piece in pieces],
        out_specs=pl.BlockSpec((tokens, block), lambda i: (0, i)),
        out_shape=jax.ShapeDtypeStruct((tokens, width), jnp.bfloat16),
        compiler_params=with_vmem(48),
        cost_estimate=pl.CostEstimate(
            flops=0, bytes_accessed=4 * tokens * width, transcendentals=0
        ),
        name="collect",
    )(*pieces)


def ring_steps(array, axis):
    groups = lax.axis_size(axis)
    order = ring_order(groups)
    onward = list(zip(order, order[1:] + order[:1]))
    back = [(to, at) for at, to in onward]
    behind, ahead, middle = [array], [array], []

    def step(after):
        one, two = behind[-1], ahead[-1]
        if after is not None:
            one, two, after = lax.optimization_barrier((one, two, after))
        if len(behind) <= (groups - 1) // 2:
            behind.append(lax.ppermute(one, axis, onward))
            ahead.append(lax.ppermute(two, axis, back))
        elif groups % 2 == 0 and not middle:
            half = array.shape[0] // 2
            middle.append(lax.ppermute(one[:half], axis, onward))
            middle.append(lax.ppermute(two[half:], axis, back))
        return after

    def done():
        return [array, *ahead[1:], *middle, *behind[:0:-1]]

    return step, done


def unpack_kernel(count, at_ref, *refs):
    pieces, outputs, order = refs[:count], refs[count:-1], refs[-1]
    groups, part, _ = pieces[0].shape
    for group in range(groups):
        slot = ring_place(group, groups) - ring_place(at_ref[1], groups) + groups
        for turn, piece in enumerate(pieces):
            order[slot % groups * count + (at_ref[0] ^ turn)] = piece[group]
    low = 0
    for out_ref in outputs:
        rows = out_ref.shape[0]
        for start in range(0, rows, 128):
            high = min(start + 128, rows)
            tokens = order[:, :, low + start : low + high].reshape(-1, high - start)
            out_ref[start:high] = tokens.T
        low += rows


def unpack(pieces, row_counts, place):
    groups, part, rows = pieces[0].shape
    tokens = groups * part * len(pieces)
    vmem = pl.BlockSpec(memory_space=pltpu.VMEM)
    return pl.pallas_call(
        functools.partial(unpack_kernel, len(pieces)),
        in_specs=[pl.BlockSpec(memory_space=pltpu.SMEM)] + [vmem] * len(pieces),
        out_specs=[vmem] * len(row_counts),
        out_shape=[jax.ShapeDtypeStruct((count, tokens), jnp.bfloat16) for count in row_counts],
        scratch_shapes=[pltpu.VMEM((groups * len(pieces), part, rows), jnp.bfloat16)],
        compiler_params=with_vmem(28),
        cost_estimate=pl.CostEstimate(
            flops=0, bytes_accessed=4 * tokens * rows, transcendentals=0
        ),
        name="unpack",
    )(place, *pieces)


def adam_kernel(strip, c_ref, x_ref, w_ref, m_ref, v_ref, *refs):
    power_ref, step_ref, first_ref, square_ref = refs[-4:]
    rows = c_ref.shape[0]
    width = x_ref.shape[1]
    lhs = c_ref[...]
    power = jnp.zeros((rows, 128), jnp.float32)
    for start in range(0, width, strip):
        at = slice(start, start + strip)
        grad = jnp.dot(lhs, x_ref[:, at], preferred_element_type=jnp.float32)
        first = beta_one * m_ref[:, at].astype(jnp.float32) + (1.0 - beta_one) * grad
        square = beta_two * v_ref[:, at].astype(jnp.float32) + (1.0 - beta_two) * grad * grad
        root = square * lax.rsqrt(square) + eps_adam
        inverse = pl.reciprocal(root, approx=True)
        inverse = inverse * (2.0 - root * inverse)
        step = w_ref[:, at].astype(jnp.float32) - rate * first * inverse
        first_ref[:, at] = first.astype(jnp.bfloat16)
        square_ref[:, at] = square.astype(jnp.bfloat16)
        step_ref[:, at] = step
        for lane in range(0, strip, 128):
            piece = step[:, lane : lane + 128]
            power += piece * piece
    power_ref[...] = jnp.sum(power.T, axis=0, keepdims=True)


def adam_pass(cotangent, inputs, state, low, made):
    rows, tokens = cotangent.shape
    total, width = state[0].shape
    block = row_block(total)
    shift = low // block
    tile = pl.BlockSpec((block, width), lambda i: (i + shift, 0))
    return pl.pallas_call(
        functools.partial(adam_kernel, strip_of(width)),
        grid=(rows // block,),
        in_specs=[
            pl.BlockSpec((block, tokens), lambda i: (i, 0)),
            pl.BlockSpec((tokens, width), lambda i: (0, 0), pipeline_mode=pl.Buffered(1)),
            tile,
            tile,
            tile,
        ]
        + [pl.BlockSpec(memory_space=pl.ANY)] * len(made),
        out_specs=[
            pl.BlockSpec((1, block), lambda i: (0, i)),
            pl.BlockSpec((block, width), lambda i: (i, 0)),
            tile,
            tile,
        ],
        out_shape=[
            jax.ShapeDtypeStruct((1, rows), jnp.float32),
            jax.ShapeDtypeStruct((rows, width), jnp.float32),
            jax.ShapeDtypeStruct((total, width), jnp.bfloat16),
            jax.ShapeDtypeStruct((total, width), jnp.bfloat16),
        ],
        input_output_aliases={5 + at: 2 + at for at in range(len(made))},
        compiler_params=with_vmem(48),
        cost_estimate=pl.CostEstimate(
            flops=2 * tokens * rows * width,
            bytes_accessed=14 * rows * width + 2 * tokens * (rows + width),
            transcendentals=0,
        ),
        name="adam",
    )(cotangent, inputs, *state, *made)


def finish_kernel(count, whole_width, step_ref, *refs):
    out_ref = refs[-1]
    power = refs[0][...]
    for other in refs[1:count]:
        power = power + other[...]
    scale = 1.0 / jnp.sqrt(power / whole_width + eps_norm)
    scale = jnp.broadcast_to(scale, (128, scale.shape[1])).T
    for lane in range(0, step_ref.shape[1], 128):
        at = slice(lane, lane + 128)
        out_ref[:, at] = (step_ref[:, at] * scale).astype(jnp.bfloat16)


def finish_rows(step, powers, whole_width, total, low, made):
    rows, width = step.shape
    block = row_block(total)
    shift = low // block
    return pl.pallas_call(
        functools.partial(finish_kernel, len(powers), whole_width),
        grid=(rows // block,),
        in_specs=[pl.BlockSpec((block, width), lambda i: (i, 0))]
        + [pl.BlockSpec((1, block), lambda i: (0, i))] * len(powers)
        + [pl.BlockSpec(memory_space=pl.ANY)] * len(made),
        out_specs=[pl.BlockSpec((block, width), lambda i: (i + shift, 0))],
        out_shape=[jax.ShapeDtypeStruct((total, width), jnp.bfloat16)],
        input_output_aliases={1 + len(powers) + at: at for at in range(len(made))},
        compiler_params=with_vmem(24),
        cost_estimate=pl.CostEstimate(
            flops=rows * width, bytes_accessed=6 * rows * width, transcendentals=0
        ),
        name="finish",
    )(step, *powers, *made)


def from_others(array, axis):
    size = lax.axis_size(axis)
    bit = size // 2
    got = {0: array}
    while bit:
        for turn in list(got):
            got[turn ^ bit] = lax.ppermute(got[turn], axis, [(at, at ^ bit) for at in range(size)])
        bit //= 2
    return [got[turn] for turn in range(size)]


def per_device(
    layer_input,
    query_cotangent,
    key_cotangent,
    up_cotangent,
    query_weight,
    key_weight,
    up_weight,
    moment_query,
    moment_key,
    moment_up,
    second_query,
    second_key,
    second_up,
):
    groups = lax.axis_size("dp")
    cols = lax.axis_size("col")
    part = layer_input.shape[0] // cols
    whole_width = layer_input.shape[1] * cols
    states = (
        (query_weight, moment_query, second_query),
        (key_weight, moment_key, second_key),
        (up_weight, moment_up, second_up),
    )
    plan = chunk_plan([state[0].shape[0] for state in states])
    place = jnp.stack([lax.axis_index("col"), lax.axis_index("dp")]).astype(jnp.int32)
    packed = pack((query_cotangent, key_cotangent, up_cotangent), plan, groups, part, place)
    step, ring = ring_steps(layer_input, "dp")
    step(None)
    owned = []
    for array in packed:
        if owned:
            array, owned[-1] = lax.optimization_barrier((array, owned[-1]))
        owned.append(lax.all_to_all(array, "dp", split_axis=0, concat_axis=0, tiled=True))
        owned[-1] = step(owned[-1])
    for _ in range(groups):
        step(None)
    gathered = collect(ring())
    moments = [[], [], []]
    updated = [[], [], []]
    for array, pieces in zip(owned, plan):
        every = unpack(from_others(array, "col"), [high - low for _, low, high in pieces], place)
        for (which, low, high), cotangent in zip(pieces, every):
            power, new, *moments[which] = adam_pass(
                cotangent, gathered, states[which], low, moments[which]
            )
            powers = from_others(power, "col")
            updated[which] = finish_rows(
                new, powers, whole_width, states[which][0].shape[0], low, updated[which]
            )
    return (
        *(made[0] for made in updated),
        *(made[0] for made in moments),
        *(made[1] for made in moments),
    )


def solution(mesh):
    tokens_split = P("dp", None)
    split = P("dp", "col")
    return jax.shard_map(
        per_device,
        mesh=mesh,
        in_specs=(split, *(tokens_split,) * 3, *(split,) * 9),
        out_specs=(split,) * 9,
        check_vma=False,
    )
```

```python
import functools

import jax
import jax.numpy as jnp
from jax import lax
from jax.experimental import pallas as pl
from jax.experimental.pallas import tpu as pltpu
from jax.sharding import PartitionSpec as P

beta_one = 0.9
beta_two = 0.95
rate = 0.1
eps_adam = 1e-08
eps_norm = 1e-06


def with_vmem(mebibytes):
    return pltpu.CompilerParams(vmem_limit_bytes=mebibytes * 1024 * 1024)


def row_block(rows, largest=256):
    for block in range(largest, 0, -128):
        if rows % block == 0:
            return block
    return rows


def chunk_plan(totals):
    first = [(which, 0, total) for which, total in enumerate(totals[:-1])]
    up = len(totals) - 1
    block = row_block(totals[up])
    blocks = max(0, (sum(totals) // 2 - sum(totals[:-1])) // block)
    if blocks:
        first.append((up, 0, blocks * block))
    return [first, [(up, blocks * block, totals[up])]]


def ring_order(groups):
    return [*range(0, groups, 2), *range(groups - 1 - groups % 2, 0, -2)]


def ring_place(at, groups):
    return jnp.where(at % 2 == 0, at // 2, groups - 1 - at // 2)


def pack_kernel(plan, groups, at_ref, *refs):
    inputs, outputs = refs[: -len(plan)], refs[-len(plan) :]
    for pieces, out_ref in zip(plan, outputs):
        start = 0
        for which, low, high in pieces:
            ref = inputs[which]
            rows = ref.shape[1] // groups
            for group in range(groups):
                out_ref[group, :, start : start + high - low] = ref[
                    :, group * rows + low : group * rows + high
                ]
            start += high - low


def pack(cotangents, plan, groups, part, place):
    outs = [
        jax.ShapeDtypeStruct(
            (groups, part, sum(high - low for _, low, high in pieces)), jnp.bfloat16
        )
        for pieces in plan
    ]
    return pl.pallas_call(
        functools.partial(pack_kernel, plan, groups),
        grid_spec=pltpu.PrefetchScalarGridSpec(
            num_scalar_prefetch=1,
            grid=(1,),
            in_specs=[
                pl.BlockSpec((part, array.shape[1]), lambda i, at: (at[0], 0))
                for array in cotangents
            ],
            out_specs=[pl.BlockSpec(out.shape, lambda i, at: (0, 0, 0)) for out in outs],
        ),
        out_shape=outs,
        compiler_params=with_vmem(16),
        cost_estimate=pl.CostEstimate(
            flops=0,
            bytes_accessed=4 * part * sum(array.shape[1] for array in cotangents),
            transcendentals=0,
        ),
        name="pack",
    )(place, *(pltpu.with_memory_space_constraint(array, pltpu.HBM) for array in cotangents))


def ring_steps(array, axis):
    groups = lax.axis_size(axis)
    order = ring_order(groups)
    onward = list(zip(order, order[1:] + order[:1]))
    back = [(to, at) for at, to in onward]
    behind, ahead, middle = [array], [array], []

    def step(after):
        one, two = behind[-1], ahead[-1]
        if after is not None:
            one, two, after = lax.optimization_barrier((one, two, after))
        if len(behind) <= (groups - 1) // 2:
            behind.append(lax.ppermute(one, axis, onward))
            ahead.append(lax.ppermute(two, axis, back))
        elif groups % 2 == 0 and not middle:
            half = array.shape[0] // 2
            middle.append(lax.ppermute(one[:half], axis, onward))
            middle.append(lax.ppermute(two[half:], axis, back))
        return after

    def done():
        return [array, *ahead[1:], *middle, *behind[:0:-1]]

    return step, done


def unpack_kernel(count, at_ref, *refs):
    pieces, outputs, order = refs[:count], refs[count:-1], refs[-1]
    groups, part, _ = pieces[0].shape
    for group in range(groups):
        slot = ring_place(group, groups) - ring_place(at_ref[1], groups) + groups
        for turn, piece in enumerate(pieces):
            order[slot % groups * count + (at_ref[0] ^ turn)] = piece[group]
    low = 0
    for out_ref in outputs:
        rows = out_ref.shape[0]
        for start in range(0, rows, 128):
            high = min(start + 128, rows)
            tokens = order[:, :, low + start : low + high].reshape(-1, high - start)
            out_ref[start:high] = tokens.T
        low += rows


def unpack(pieces, row_counts, place):
    groups, part, rows = pieces[0].shape
    tokens = groups * part * len(pieces)
    vmem = pl.BlockSpec(memory_space=pltpu.VMEM)
    return pl.pallas_call(
        functools.partial(unpack_kernel, len(pieces)),
        in_specs=[pl.BlockSpec(memory_space=pltpu.SMEM)] + [vmem] * len(pieces),
        out_specs=[vmem] * len(row_counts),
        out_shape=[pltpu.VMEM((count, tokens), jnp.bfloat16) for count in row_counts],
        scratch_shapes=[pltpu.VMEM((groups * len(pieces), part, rows), jnp.bfloat16)],
        compiler_params=with_vmem(12),
        cost_estimate=pl.CostEstimate(
            flops=0, bytes_accessed=4 * tokens * rows, transcendentals=0
        ),
        name="unpack",
    )(place, *pieces)


def preload_kernel(*refs):
    count = (len(refs) - 3) // 2
    token, sems = refs[-2:]
    outputs = refs[count + 1 :]
    copies = [pltpu.make_async_copy(refs[at], outputs[at], sems.at[at]) for at in range(count)]
    token[...] = jnp.zeros_like(token)
    for copy in copies:
        copy.start()
    for copy in copies:
        copy.wait()


def preload(arrays, after):
    return pl.pallas_call(
        preload_kernel,
        in_specs=[pl.BlockSpec(memory_space=pl.ANY)] * (len(arrays) + 1),
        out_specs=[pl.BlockSpec(memory_space=pltpu.VMEM)] * (len(arrays) + 1),
        out_shape=[pltpu.VMEM(array.shape, array.dtype) for array in arrays]
        + [jax.ShapeDtypeStruct((8, 128), jnp.float32)],
        scratch_shapes=[pltpu.SemaphoreType.DMA((len(arrays),))],
        compiler_params=with_vmem(4),
        cost_estimate=pl.CostEstimate(
            flops=0, bytes_accessed=sum(2 * array.size for array in arrays), transcendentals=0
        ),
        name="preload",
    )(*(pltpu.with_memory_space_constraint(array, pltpu.HBM) for array in arrays), after)


def write_back(buffers, outputs, sems, slot, at):
    return [
        pltpu.make_async_copy(buffer.at[slot, : at.size], out.at[at], sems.at[slot, which])
        for which, (buffer, out) in enumerate(zip(buffers, outputs))
    ]


def over_blocks(count, body):
    if count == 1:
        body(0)
    else:
        pl.loop(0, count)(body)


def update_tile(grad, weight, moment, second):
    first = beta_one * moment.astype(jnp.float32) + (1.0 - beta_one) * grad
    square = beta_two * second.astype(jnp.float32) + (1.0 - beta_two) * grad * grad
    root = square * lax.rsqrt(square) + eps_adam
    inverse = pl.reciprocal(root, approx=True)
    inverse = inverse * (2.0 - root * inverse)
    return first, square, weight.astype(jnp.float32) - rate * first * inverse


def adam_kernel(strip, count_x, cuts, *refs):
    refs = list(refs)
    take = lambda count: [refs.pop(0) for _ in range(count)]
    x_refs = take(count_x)
    ins = [(take(len(cut)), *take(3)) for cut in cuts]
    power_ref = refs.pop(0)
    outs = [take(4) for _ in cuts]
    grads, buffers, power_sum, sems = (refs[0], refs[1]), (refs[2], refs[3]), refs[4], refs[5]
    width = x_refs[0].shape[1]
    strips = width // strip
    base = 0
    for cut, (c_refs, w_ref, m_ref, v_ref), (hi_ref, lo_ref, *moments) in zip(cuts, ins, outs):
        low = 0
        for c_ref, rows in zip(c_refs, cut):
            block = row_block(rows)
            count = rows // block

            def multiply(at, which, c_ref=c_ref, block=block):
                lhs = c_ref[pl.ds(at * block, block), :]
                columns = slice(which * strip, (which + 1) * strip)
                rhs = jnp.concatenate([x_ref[:, columns] for x_ref in x_refs], axis=0)
                grads[which % 2][:block] = jnp.dot(lhs, rhs, preferred_element_type=jnp.float32)

            def one_block(at, low=low, base=base, count=count, block=block, multiply=multiply):
                slot = at % 2
                place = pl.ds(low + at * block, block)
                if count > 2:

                    @pl.when(at >= 2)
                    def _():
                        for copy in write_back(buffers, moments, sems, slot, place):
                            copy.wait()

                for which in range(strips):
                    if which + 1 < strips:
                        multiply(at, which + 1)
                    elif count > 1:
                        multiply(jnp.minimum(at + 1, count - 1), 0)
                    columns = slice(which * strip, (which + 1) * strip)
                    for row in range(0, block, 16):
                        inside = slice(row, row + 16)
                        tile = pl.ds(low + at * block + row, 16)
                        first, square, step = update_tile(
                            grads[which % 2][inside],
                            w_ref[tile, columns],
                            m_ref[tile, columns],
                            v_ref[tile, columns],
                        )
                        buffers[0][slot, inside, columns] = first.astype(jnp.bfloat16)
                        buffers[1][slot, inside, columns] = square.astype(jnp.bfloat16)
                        hi = step.astype(jnp.bfloat16)
                        hi_ref[tile, columns] = hi
                        lo_ref[tile, columns] = (step - hi.astype(jnp.float32)).astype(
                            jnp.bfloat16
                        )
                        power = step[:, :128] * step[:, :128]
                        for lane in range(128, strip, 128):
                            power += step[:, lane : lane + 128] * step[:, lane : lane + 128]
                        if which:
                            power += power_sum[inside]
                        power_sum[inside] = power
                power_ref[:, pl.ds(base + low + at * block, block)] = jnp.sum(
                    power_sum[:block].T, axis=0, keepdims=True
                )
                for copy in write_back(buffers, moments, sems, slot, place):
                    copy.start()

            multiply(0, 0)
            over_blocks(count, one_block)
            for at in range(max(0, count - 2), count):
                place = pl.ds(low + at * block, block)
                for copy in write_back(buffers, moments, sems, at % 2, place):
                    copy.wait()
            low += rows
        base += low


def strip_of(width, largest=512):
    for strip in range(largest, 0, -128):
        if width % (2 * strip) == 0:
            return strip


def adam_pass(x_pieces, cotangents, states):
    width = x_pieces[0].shape[1]
    tokens = cotangents[0][0].shape[1]
    strip = strip_of(width)
    cuts = [[piece.shape[0] for piece in pieces] for pieces in cotangents]
    rows = sum(sum(cut) for cut in cuts)
    block = max(row_block(count) for cut in cuts for count in cut)
    args, aliases, outs = list(x_pieces), {}, []
    for pieces, state in zip(cotangents, states):
        args += pieces
        aliases[len(args)] = len(outs) + 1
        aliases[len(args) + 1] = len(outs) + 2
        args += state
        shape = state[0].shape
        outs += [pltpu.VMEM(shape, jnp.bfloat16)] * 2
        outs += [jax.ShapeDtypeStruct(shape, jnp.bfloat16)] * 2
    vmem = pl.BlockSpec(memory_space=pltpu.VMEM)
    hbm = pl.BlockSpec(memory_space=pl.ANY)
    done = pl.pallas_call(
        functools.partial(adam_kernel, strip, len(x_pieces), cuts),
        in_specs=[vmem] * len(args),
        out_specs=[vmem] + [vmem, vmem, hbm, hbm] * len(states),
        out_shape=[jax.ShapeDtypeStruct((1, rows), jnp.float32), *outs],
        input_output_aliases=aliases,
        scratch_shapes=[
            pltpu.VMEM((block, strip), jnp.float32),
            pltpu.VMEM((block, strip), jnp.float32),
            pltpu.VMEM((2, block, width), jnp.bfloat16),
            pltpu.VMEM((2, block, width), jnp.bfloat16),
            pltpu.VMEM((block, 128), jnp.float32),
            pltpu.SemaphoreType.DMA((2, 2)),
        ],
        compiler_params=with_vmem(12),
        cost_estimate=pl.CostEstimate(
            flops=2 * tokens * rows * width, bytes_accessed=4 * rows * width, transcendentals=0
        ),
        name="adam",
    )(*(pltpu.with_memory_space_constraint(array, pltpu.VMEM) for array in args))
    return done[0], [done[at : at + 4] for at in range(1, len(done), 4)]


def finish_kernel(count, whole_width, matrices, *refs):
    powers, refs = refs[:count], refs[count:]
    parts, outputs, (buffer, sems) = refs[: 2 * matrices], refs[2 * matrices : -2], refs[-2:]
    base = 0
    for which, out_ref in enumerate(outputs):
        hi_ref, lo_ref = parts[2 * which : 2 * which + 2]
        rows, width = hi_ref.shape
        block = row_block(rows)
        total = rows // block

        def one_block(at, base=base, block=block, total=total):
            slot = at % 2
            place = pl.ds(at * block, block)
            if total > 2:

                @pl.when(at >= 2)
                def _():
                    for copy in write_back([buffer], [out_ref], sems, slot, place):
                        copy.wait()

            lanes = pl.ds(base + at * block, block)
            power = powers[0][:, lanes]
            for other in powers[1:]:
                power = power + other[:, lanes]
            scale = 1.0 / jnp.sqrt(power / whole_width + eps_norm)
            scale = jnp.broadcast_to(scale, (128, block)).T
            for row in range(0, block, 16):
                inside = slice(row, row + 16)
                tile = pl.ds(at * block + row, 16)
                for lane in range(0, width, 128):
                    columns = slice(lane, lane + 128)
                    step = hi_ref[tile, columns].astype(jnp.float32)
                    step = step + lo_ref[tile, columns].astype(jnp.float32)
                    buffer[slot, inside, columns] = (step * scale[inside]).astype(jnp.bfloat16)
            for copy in write_back([buffer], [out_ref], sems, slot, place):
                copy.start()

        over_blocks(total, one_block)
        for at in range(max(0, total - 2), total):
            place = pl.ds(at * block, block)
            for copy in write_back([buffer], [out_ref], sems, at % 2, place):
                copy.wait()
        base += rows


def finish_rows(parts, powers, whole_width):
    shapes = [array.shape for array in parts[::2]]
    width = shapes[0][1]
    block = max(row_block(shape[0]) for shape in shapes)
    vmem = pl.BlockSpec(memory_space=pltpu.VMEM)
    return pl.pallas_call(
        functools.partial(finish_kernel, len(powers), whole_width, len(shapes)),
        in_specs=[vmem] * (len(powers) + len(parts)),
        out_specs=[pl.BlockSpec(memory_space=pl.ANY)] * len(shapes),
        out_shape=[jax.ShapeDtypeStruct(shape, jnp.bfloat16) for shape in shapes],
        scratch_shapes=[
            pltpu.VMEM((2, block, width), jnp.bfloat16),
            pltpu.SemaphoreType.DMA((2, 1)),
        ],
        compiler_params=with_vmem(8),
        cost_estimate=pl.CostEstimate(
            flops=sum(2 * rows * width for rows, _ in shapes),
            bytes_accessed=sum(2 * rows * width for rows, _ in shapes),
            transcendentals=0,
        ),
        name="finish",
    )(*powers, *(pltpu.with_memory_space_constraint(array, pltpu.VMEM) for array in parts))


def from_others(array, axis):
    size = lax.axis_size(axis)
    bit = size // 2
    got = {0: array}
    while bit:
        for turn in list(got):
            got[turn ^ bit] = lax.ppermute(got[turn], axis, [(at, at ^ bit) for at in range(size)])
        bit //= 2
    return [got[turn] for turn in range(size)]


def per_device(
    layer_input,
    query_cotangent,
    key_cotangent,
    up_cotangent,
    query_weight,
    key_weight,
    up_weight,
    moment_query,
    moment_key,
    moment_up,
    second_query,
    second_key,
    second_up,
):
    groups = lax.axis_size("dp")
    cols = lax.axis_size("col")
    part = layer_input.shape[0] // cols
    whole_width = layer_input.shape[1] * cols
    states = (
        (query_weight, moment_query, second_query),
        (key_weight, moment_key, second_key),
        (up_weight, moment_up, second_up),
    )
    plan = chunk_plan([state[0].shape[0] for state in states])
    place = jnp.stack([lax.axis_index("col"), lax.axis_index("dp")]).astype(jnp.int32)
    packed = pack((query_cotangent, key_cotangent, up_cotangent), plan, groups, part, place)
    *held, loaded = preload([array for state in states for array in state], packed[0])
    held = [held[at : at + 3] for at in range(0, len(held), 3)]
    step, ring = ring_steps(layer_input, "dp")
    step(None)
    owned = []
    for array in packed:
        if owned:
            array, owned[-1] = lax.optimization_barrier((array, owned[-1]))
        owned.append(lax.all_to_all(array, "dp", split_axis=0, concat_axis=0, tiled=True))
        owned[-1], loaded = step((owned[-1], loaded))
    for _ in range(groups):
        step(None)
    cotangents = [[], [], []]
    for array, pieces in zip(owned, plan):
        every = unpack(from_others(array, "col"), [high - low for _, low, high in pieces], place)
        for (which, _, _), cotangent in zip(pieces, every):
            cotangents[which].append(cotangent)
    updated = [None] * 3
    moments = [None] * 3
    passes = []
    for group in ((2,), (0, 1)):
        power, made = adam_pass(
            ring(), [cotangents[which] for which in group], [held[which] for which in group]
        )
        passes.append((group, from_others(power, "col"), made))
    for group, powers, made in passes:
        parts = [array for done in made for array in done[:2]]
        for which, done, array in zip(group, made, finish_rows(parts, powers, whole_width)):
            updated[which] = array
            moments[which] = done[2:]
    return (*updated, *(done[0] for done in moments), *(done[1] for done in moments))


def solution(mesh):
    tokens_split = P("dp", None)
    split = P("dp", "col")
    return jax.shard_map(
        per_device,
        mesh=mesh,
        in_specs=(split, *(tokens_split,) * 3, *(split,) * 9),
        out_specs=(split,) * 9,
        check_vma=False,
    )
```

```python
import functools

import jax
import jax.numpy as jnp
from jax import lax
from jax.experimental import pallas as pl
from jax.experimental.pallas import tpu as pltpu
from jax.sharding import PartitionSpec as P

beta_one = 0.9
beta_two = 0.95
rate = 0.1
eps_adam = 1e-08
eps_norm = 1e-06


def with_vmem(mebibytes):
    return pltpu.CompilerParams(vmem_limit_bytes=mebibytes * 1024 * 1024)


def row_block(rows, largest=256):
    for block in range(largest, 0, -128):
        if rows % block == 0:
            return block
    return rows


def chunk_plan(totals):
    first = [(which, 0, total) for which, total in enumerate(totals[:-1])]
    up = len(totals) - 1
    block = row_block(totals[up])
    blocks = max(0, (sum(totals) // 2 - sum(totals[:-1])) // block)
    if blocks:
        first.append((up, 0, blocks * block))
    return [first, [(up, blocks * block, totals[up])]]


def ring_order(groups):
    return [*range(0, groups, 2), *range(groups - 1 - groups % 2, 0, -2)]


def ring_place(at, groups):
    return jnp.where(at % 2 == 0, at // 2, groups - 1 - at // 2)


def pack_kernel(plan, groups, at_ref, *refs):
    inputs, outputs = refs[: -len(plan)], refs[-len(plan) :]
    for pieces, out_ref in zip(plan, outputs):
        start = 0
        for which, low, high in pieces:
            ref = inputs[which]
            rows = ref.shape[1] // groups
            for group in range(groups):
                out_ref[group, :, start : start + high - low] = ref[
                    :, group * rows + low : group * rows + high
                ]
            start += high - low


def pack(cotangents, plan, groups, part, place):
    outs = [
        jax.ShapeDtypeStruct(
            (groups, part, sum(high - low for _, low, high in pieces)), jnp.bfloat16
        )
        for pieces in plan
    ]
    return pl.pallas_call(
        functools.partial(pack_kernel, plan, groups),
        grid_spec=pltpu.PrefetchScalarGridSpec(
            num_scalar_prefetch=1,
            grid=(1,),
            in_specs=[
                pl.BlockSpec((part, array.shape[1]), lambda i, at: (at[0], 0))
                for array in cotangents
            ],
            out_specs=[pl.BlockSpec(out.shape, lambda i, at: (0, 0, 0)) for out in outs],
        ),
        out_shape=outs,
        compiler_params=with_vmem(16),
        cost_estimate=pl.CostEstimate(
            flops=0,
            bytes_accessed=4 * part * sum(array.shape[1] for array in cotangents),
            transcendentals=0,
        ),
        name="pack",
    )(place, *(pltpu.with_memory_space_constraint(array, pltpu.HBM) for array in cotangents))


def ring_steps(array, axis):
    groups = lax.axis_size(axis)
    order = ring_order(groups)
    onward = list(zip(order, order[1:] + order[:1]))
    back = [(to, at) for at, to in onward]
    behind, ahead, middle = [array], [array], []

    def step(after=()):
        one, two = behind[-1], ahead[-1]
        if after:
            one, two = join((one, two), after)
            behind[-1], ahead[-1] = one, two
        if len(behind) <= (groups - 1) // 2:
            behind.append(lax.ppermute(one, axis, onward))
            ahead.append(lax.ppermute(two, axis, back))
        elif groups % 2 == 0 and not middle:
            half = array.shape[0] // 2
            middle.append(lax.ppermute(one[:half], axis, onward))
            middle.append(lax.ppermute(two[half:], axis, back))
        return behind[-1], ahead[-1]

    def done():
        return [array, *ahead[1:], *middle, *behind[:0:-1]]

    return step, done


def unpack_kernel(count, at_ref, *refs):
    pieces, outputs, order = refs[:count], refs[count:-1], refs[-1]
    groups, part, _ = pieces[0].shape
    for group in range(groups):
        slot = ring_place(group, groups) - ring_place(at_ref[1], groups) + groups
        for turn, piece in enumerate(pieces):
            order[slot % groups * count + (at_ref[0] ^ turn)] = piece[group]
    low = 0
    for out_ref in outputs:
        rows = out_ref.shape[0]
        for start in range(0, rows, 128):
            high = min(start + 128, rows)
            tokens = order[:, :, low + start : low + high].reshape(-1, high - start)
            out_ref[start:high] = tokens.T
        low += rows


def unpack(pieces, row_counts, place):
    groups, part, rows = pieces[0].shape
    tokens = groups * part * len(pieces)
    vmem = pl.BlockSpec(memory_space=pltpu.VMEM)
    return pl.pallas_call(
        functools.partial(unpack_kernel, len(pieces)),
        in_specs=[pl.BlockSpec(memory_space=pltpu.SMEM)] + [vmem] * len(pieces),
        out_specs=[vmem] * len(row_counts),
        out_shape=[pltpu.VMEM((count, tokens), jnp.bfloat16) for count in row_counts],
        scratch_shapes=[pltpu.VMEM((groups * len(pieces), part, rows), jnp.bfloat16)],
        compiler_params=with_vmem(12),
        cost_estimate=pl.CostEstimate(
            flops=0, bytes_accessed=4 * tokens * rows, transcendentals=0
        ),
        name="unpack",
    )(place, *pieces)


def join_kernel(*refs):
    pass


def join(arrays, after):
    count = len(arrays)
    hbm = pl.BlockSpec(memory_space=pl.ANY)
    return pl.pallas_call(
        join_kernel,
        in_specs=[hbm] * (count + len(after)),
        out_specs=[hbm] * count,
        out_shape=[jax.ShapeDtypeStruct(array.shape, array.dtype) for array in arrays],
        input_output_aliases={at: at for at in range(count)},
        compiler_params=with_vmem(1),
        name="join",
    )(*arrays, *after)


def preload_kernel(*refs):
    count = (len(refs) - 2) // 2
    token, sems = refs[-2:]
    outputs = refs[count:]
    copies = [pltpu.make_async_copy(refs[at], outputs[at], sems.at[at]) for at in range(count)]
    token[...] = jnp.zeros_like(token)
    for copy in copies:
        copy.start()
    for copy in copies:
        copy.wait()


def preload(arrays):
    return pl.pallas_call(
        preload_kernel,
        in_specs=[pl.BlockSpec(memory_space=pl.ANY)] * len(arrays),
        out_specs=[pl.BlockSpec(memory_space=pltpu.VMEM)] * (len(arrays) + 1),
        out_shape=[pltpu.VMEM(array.shape, array.dtype) for array in arrays]
        + [jax.ShapeDtypeStruct((8, 128), jnp.float32)],
        scratch_shapes=[pltpu.SemaphoreType.DMA((len(arrays),))],
        compiler_params=with_vmem(4),
        cost_estimate=pl.CostEstimate(
            flops=0, bytes_accessed=sum(2 * array.size for array in arrays), transcendentals=0
        ),
        name="preload",
    )(*(pltpu.with_memory_space_constraint(array, pltpu.HBM) for array in arrays))


def write_back(buffers, outputs, sems, slot, at):
    return [
        pltpu.make_async_copy(buffer.at[slot, : at.size], out.at[at], sems.at[slot, which])
        for which, (buffer, out) in enumerate(zip(buffers, outputs))
    ]


def over_blocks(count, body):
    if count == 1:
        body(0)
    else:
        pl.loop(0, count)(body)


def update_tile(grad, weight, moment, second):
    first = beta_one * moment.astype(jnp.float32) + (1.0 - beta_one) * grad
    square = beta_two * second.astype(jnp.float32) + (1.0 - beta_two) * grad * grad
    inverse = lax.rsqrt(square)
    root = square * inverse + eps_adam
    inverse = inverse * (2.0 - root * inverse)
    return first, square, weight.astype(jnp.float32) - rate * first * inverse


def adam_kernel(strip, count_x, cuts, *refs):
    refs = list(refs)
    take = lambda count: [refs.pop(0) for _ in range(count)]
    x_refs = take(count_x)
    ins = [(take(len(cut)), *take(3)) for cut in cuts]
    power_ref = refs.pop(0)
    outs = [take(4) for _ in cuts]
    grads, buffers, power_sum, sems = (refs[0], refs[1]), (refs[2], refs[3]), refs[4], refs[5]
    width = x_refs[0].shape[1]
    strips = width // strip
    base = 0
    for cut, (c_refs, w_ref, m_ref, v_ref), (hi_ref, lo_ref, *moments) in zip(cuts, ins, outs):
        low = 0
        for c_ref, rows in zip(c_refs, cut):
            block = row_block(rows)
            count = rows // block

            def multiply(at, which, c_ref=c_ref, block=block):
                lhs = c_ref[pl.ds(at * block, block), :]
                columns = slice(which * strip, (which + 1) * strip)
                rhs = jnp.concatenate([x_ref[:, columns] for x_ref in x_refs], axis=0)
                grads[which % 2][:block] = jnp.dot(lhs, rhs, preferred_element_type=jnp.float32)

            def one_block(at, low=low, base=base, count=count, block=block, multiply=multiply):
                slot = at % 2
                place = pl.ds(low + at * block, block)
                if count > 2:

                    @pl.when(at >= 2)
                    def _():
                        for copy in write_back(buffers, moments, sems, slot, place):
                            copy.wait()

                for which in range(strips):
                    if which + 1 < strips:
                        multiply(at, which + 1)
                    elif count > 1:
                        multiply(jnp.minimum(at + 1, count - 1), 0)
                    columns = slice(which * strip, (which + 1) * strip)
                    for row in range(0, block, 16):
                        inside = slice(row, row + 16)
                        tile = pl.ds(low + at * block + row, 16)
                        first, square, step = update_tile(
                            grads[which % 2][inside],
                            w_ref[tile, columns],
                            m_ref[tile, columns],
                            v_ref[tile, columns],
                        )
                        buffers[0][slot, inside, columns] = first.astype(jnp.bfloat16)
                        buffers[1][slot, inside, columns] = square.astype(jnp.bfloat16)
                        hi = step.astype(jnp.bfloat16)
                        hi_ref[tile, columns] = hi
                        lo_ref[tile, columns] = (step - hi.astype(jnp.float32)).astype(
                            jnp.bfloat16
                        )
                        power = step[:, :128] * step[:, :128]
                        for lane in range(128, strip, 128):
                            power += step[:, lane : lane + 128] * step[:, lane : lane + 128]
                        if which:
                            power += power_sum[inside]
                        power_sum[inside] = power
                power_ref[:, pl.ds(base + low + at * block, block)] = jnp.sum(
                    power_sum[:block].T, axis=0, keepdims=True
                )
                for copy in write_back(buffers, moments, sems, slot, place):
                    copy.start()

            multiply(0, 0)
            over_blocks(count, one_block)
            for at in range(max(0, count - 2), count):
                place = pl.ds(low + at * block, block)
                for copy in write_back(buffers, moments, sems, at % 2, place):
                    copy.wait()
            low += rows
        base += low


def strip_of(width, largest=256):
    for strip in range(largest, 0, -128):
        if width % (2 * strip) == 0:
            return strip


def adam_pass(x_pieces, cotangents, states):
    width = x_pieces[0].shape[1]
    tokens = cotangents[0][0].shape[1]
    strip = strip_of(width)
    cuts = [[piece.shape[0] for piece in pieces] for pieces in cotangents]
    rows = sum(sum(cut) for cut in cuts)
    block = max(row_block(count) for cut in cuts for count in cut)
    args, aliases, outs = list(x_pieces), {}, []
    for pieces, state in zip(cotangents, states):
        args += pieces
        aliases[len(args)] = len(outs) + 1
        aliases[len(args) + 1] = len(outs) + 2
        args += state
        shape = state[0].shape
        outs += [pltpu.VMEM(shape, jnp.bfloat16)] * 2
        outs += [jax.ShapeDtypeStruct(shape, jnp.bfloat16)] * 2
    vmem = pl.BlockSpec(memory_space=pltpu.VMEM)
    hbm = pl.BlockSpec(memory_space=pl.ANY)
    done = pl.pallas_call(
        functools.partial(adam_kernel, strip, len(x_pieces), cuts),
        in_specs=[vmem] * len(args),
        out_specs=[vmem] + [vmem, vmem, hbm, hbm] * len(states),
        out_shape=[jax.ShapeDtypeStruct((1, rows), jnp.float32), *outs],
        input_output_aliases=aliases,
        scratch_shapes=[
            pltpu.VMEM((block, strip), jnp.float32),
            pltpu.VMEM((block, strip), jnp.float32),
            pltpu.VMEM((2, block, width), jnp.bfloat16),
            pltpu.VMEM((2, block, width), jnp.bfloat16),
            pltpu.VMEM((block, 128), jnp.float32),
            pltpu.SemaphoreType.DMA((2, 2)),
        ],
        compiler_params=with_vmem(12),
        cost_estimate=pl.CostEstimate(
            flops=2 * tokens * rows * width, bytes_accessed=4 * rows * width, transcendentals=0
        ),
        name="adam",
    )(*(pltpu.with_memory_space_constraint(array, pltpu.VMEM) for array in args))
    return done[0], [done[at : at + 4] for at in range(1, len(done), 4)]


def finish_kernel(count, whole_width, matrices, *refs):
    powers, refs = refs[:count], refs[count:]
    parts, outputs, (buffer, sems) = refs[: 2 * matrices], refs[2 * matrices : -2], refs[-2:]
    slots = buffer.shape[0]
    base = 0
    for which, out_ref in enumerate(outputs):
        hi_ref, lo_ref = parts[2 * which : 2 * which + 2]
        rows, width = hi_ref.shape
        block = row_block(rows, 128)
        total = rows // block

        def one_block(at, base=base, block=block, total=total):
            slot = at % slots
            place = pl.ds(at * block, block)
            if total > slots:

                @pl.when(at >= slots)
                def _():
                    for copy in write_back([buffer], [out_ref], sems, slot, place):
                        copy.wait()

            lanes = pl.ds(base + at * block, block)
            power = powers[0][:, lanes]
            for other in powers[1:]:
                power = power + other[:, lanes]
            scale = 1.0 / jnp.sqrt(power / whole_width + eps_norm)
            scale = jnp.broadcast_to(scale, (128, block)).T
            for row in range(0, block, 16):
                inside = slice(row, row + 16)
                tile = pl.ds(at * block + row, 16)
                for lane in range(0, width, 128):
                    columns = slice(lane, lane + 128)
                    step = hi_ref[tile, columns].astype(jnp.float32)
                    step = step + lo_ref[tile, columns].astype(jnp.float32)
                    buffer[slot, inside, columns] = (step * scale[inside]).astype(jnp.bfloat16)
            for copy in write_back([buffer], [out_ref], sems, slot, place):
                copy.start()

        over_blocks(total, one_block)
        for at in range(max(0, total - slots), total):
            place = pl.ds(at * block, block)
            for copy in write_back([buffer], [out_ref], sems, at % slots, place):
                copy.wait()
        base += rows


def finish_rows(parts, powers, whole_width):
    shapes = [array.shape for array in parts[::2]]
    width = shapes[0][1]
    block = max(row_block(shape[0], 128) for shape in shapes)
    vmem = pl.BlockSpec(memory_space=pltpu.VMEM)
    return pl.pallas_call(
        functools.partial(finish_kernel, len(powers), whole_width, len(shapes)),
        in_specs=[vmem] * (len(powers) + len(parts)),
        out_specs=[pl.BlockSpec(memory_space=pl.ANY)] * len(shapes),
        out_shape=[jax.ShapeDtypeStruct(shape, jnp.bfloat16) for shape in shapes],
        scratch_shapes=[
            pltpu.VMEM((4, block, width), jnp.bfloat16),
            pltpu.SemaphoreType.DMA((4, 1)),
        ],
        compiler_params=with_vmem(8),
        cost_estimate=pl.CostEstimate(
            flops=sum(2 * rows * width for rows, _ in shapes),
            bytes_accessed=sum(2 * rows * width for rows, _ in shapes),
            transcendentals=0,
        ),
        name="finish",
    )(*powers, *(pltpu.with_memory_space_constraint(array, pltpu.VMEM) for array in parts))


def from_others(array, axis):
    size = lax.axis_size(axis)
    bit = size // 2
    got = {0: array}
    while bit:
        for turn in list(got):
            got[turn ^ bit] = lax.ppermute(got[turn], axis, [(at, at ^ bit) for at in range(size)])
        bit //= 2
    return [got[turn] for turn in range(size)]


def straight_from_others(array, axis):
    size = lax.axis_size(axis)
    return [array] + [
        lax.ppermute(array, axis, [(at, at ^ turn) for at in range(size)])
        for turn in range(1, size)
    ]


def per_device(
    layer_input,
    query_cotangent,
    key_cotangent,
    up_cotangent,
    query_weight,
    key_weight,
    up_weight,
    moment_query,
    moment_key,
    moment_up,
    second_query,
    second_key,
    second_up,
):
    groups = lax.axis_size("dp")
    cols = lax.axis_size("col")
    part = layer_input.shape[0] // cols
    whole_width = layer_input.shape[1] * cols
    states = (
        (query_weight, moment_query, second_query),
        (key_weight, moment_key, second_key),
        (up_weight, moment_up, second_up),
    )
    plan = chunk_plan([state[0].shape[0] for state in states])
    place = jnp.stack([lax.axis_index("col"), lax.axis_index("dp")]).astype(jnp.int32)
    packed = pack((query_cotangent, key_cotangent, up_cotangent), plan, groups, part, place)
    step, ring = ring_steps(layer_input, "dp")
    arrived = step()
    *held, loaded = preload([array for state in states for array in state])
    held = [held[at : at + 3] for at in range(0, len(held), 3)]
    packed = join(packed, (*arrived, loaded))
    step()
    owned = [
        lax.all_to_all(array, "dp", split_axis=0, concat_axis=0, tiled=True) for array in packed
    ]
    step(owned)
    for _ in range(groups):
        step()
    cotangents = [[], [], []]
    for array, pieces in zip(owned, plan):
        every = unpack(from_others(array, "col"), [high - low for _, low, high in pieces], place)
        for (which, _, _), cotangent in zip(pieces, every):
            cotangents[which].append(cotangent)
    updated = [None] * 3
    moments = [None] * 3
    passes = []
    for group in ((2,), (0, 1)):
        power, made = adam_pass(
            ring(), [cotangents[which] for which in group], [held[which] for which in group]
        )
        passes.append((group, straight_from_others(power, "col"), made))
    for group, powers, made in passes:
        parts = [array for done in made for array in done[:2]]
        for which, done, array in zip(group, made, finish_rows(parts, powers, whole_width)):
            updated[which] = array
            moments[which] = done[2:]
    return (*updated, *(done[0] for done in moments), *(done[1] for done in moments))


def solution(mesh):
    tokens_split = P("dp", None)
    split = P("dp", "col")
    return jax.shard_map(
        per_device,
        mesh=mesh,
        in_specs=(split, *(tokens_split,) * 3, *(split,) * 9),
        out_specs=(split,) * 9,
        check_vma=False,
    )
```

```python
import functools

import jax
import jax.numpy as jnp
from jax import lax
from jax.experimental import pallas as pl
from jax.experimental.pallas import tpu as pltpu
from jax.sharding import PartitionSpec as P

beta_one = 0.9
beta_two = 0.95
rate = 0.1
eps_adam = 1e-08
eps_norm = 1e-06


def with_vmem(mebibytes):
    return pltpu.CompilerParams(vmem_limit_bytes=mebibytes * 1024 * 1024)


def row_block(rows, largest=256):
    for block in range(largest, 0, -128):
        if rows % block == 0:
            return block
    return rows


def ring_order(groups):
    return [*range(0, groups, 2), *range(groups - 1 - groups % 2, 0, -2)]


def ring_place(at, groups):
    return jnp.where(at % 2 == 0, at // 2, groups - 1 - at // 2)


def chunk_plan(totals):
    first = [(which, 0, total) for which, total in enumerate(totals[:-1])]
    up = len(totals) - 1
    block = row_block(totals[up])
    blocks = max(0, (sum(totals) // 2 - sum(totals[:-1])) // block)
    if blocks:
        first.append((up, 0, blocks * block))
    return [first, [(up, blocks * block, totals[up])]]


def pack_kernel(plan, groups, at_ref, *refs):
    inputs, outputs = refs[: -len(plan)], refs[-len(plan) :]
    for pieces, out_ref in zip(plan, outputs):
        start = 0
        for which, low, high in pieces:
            ref = inputs[which]
            rows = ref.shape[1] // groups
            for group in range(groups):
                out_ref[group, :, start : start + high - low] = ref[
                    :, group * rows + low : group * rows + high
                ]
            start += high - low


def pack(cotangents, plan, groups, part, place):
    outs = [
        jax.ShapeDtypeStruct(
            (groups, part, sum(high - low for _, low, high in pieces)), jnp.bfloat16
        )
        for pieces in plan
    ]
    return pl.pallas_call(
        functools.partial(pack_kernel, plan, groups),
        grid_spec=pltpu.PrefetchScalarGridSpec(
            num_scalar_prefetch=1,
            grid=(1,),
            in_specs=[
                pl.BlockSpec((part, array.shape[1]), lambda i, at: (at[0], 0))
                for array in cotangents
            ],
            out_specs=[pl.BlockSpec(out.shape, lambda i, at: (0, 0, 0)) for out in outs],
        ),
        out_shape=outs,
        compiler_params=with_vmem(16),
        cost_estimate=pl.CostEstimate(
            flops=0,
            bytes_accessed=4 * part * sum(array.shape[1] for array in cotangents),
            transcendentals=0,
        ),
        name="pack",
    )(place, *(pltpu.with_memory_space_constraint(array, pltpu.HBM) for array in cotangents))


def halves_kernel(one_ref, two_ref, first_ref, last_ref):
    half = first_ref.shape[0]
    first_ref[...] = one_ref[:half]
    last_ref[...] = two_ref[half:]


def halves(one, two):
    half = jax.ShapeDtypeStruct((one.shape[0] // 2, one.shape[1]), one.dtype)
    vmem = pl.BlockSpec(memory_space=pltpu.VMEM)
    return pl.pallas_call(
        halves_kernel,
        in_specs=[vmem] * 2,
        out_specs=[vmem] * 2,
        out_shape=[half] * 2,
        compiler_params=with_vmem(4),
        cost_estimate=pl.CostEstimate(
            flops=0, bytes_accessed=4 * one.size, transcendentals=0
        ),
        name="halves",
    )(one, two)


def ring_paths(groups):
    order = ring_order(groups)
    onward = list(zip(order, order[1:] + order[:1]))
    return onward, [(to, at) for at, to in onward]


def ring_step(one, two, axis):
    onward, back = ring_paths(lax.axis_size(axis))
    return lax.ppermute(one, axis, onward), lax.ppermute(two, axis, back)


def unpack_kernel(count, at_ref, *refs):
    pieces, outputs, orders = refs[:count], refs[count:-2], refs[-2:]
    groups = pieces[0].shape[0]
    here = ring_place(at_ref[1], groups)
    slots = [(ring_place(group, groups) - here + groups) % groups for group in range(groups)]
    low = 0
    for out_ref in outputs:
        rows = out_ref.shape[0]
        for start in range(0, rows, 128):
            high = min(start + 128, rows)
            order = orders[start // 128 % 2]
            for group, slot in enumerate(slots):
                for turn, piece in enumerate(pieces):
                    order[slot * count + (at_ref[0] ^ turn), :, : high - start] = piece[
                        group, :, low + start : low + high
                    ]
            out_ref[start:high] = order[...].reshape(-1, 128).T[: high - start]
        low += rows


def unpack(pieces, row_counts, place):
    groups, part, rows = pieces[0].shape
    tokens = groups * part * len(pieces)
    vmem = pl.BlockSpec(memory_space=pltpu.VMEM)
    order = pltpu.VMEM((groups * len(pieces), part, 128), jnp.bfloat16)
    return pl.pallas_call(
        functools.partial(unpack_kernel, len(pieces)),
        in_specs=[pl.BlockSpec(memory_space=pltpu.SMEM)] + [vmem] * len(pieces),
        out_specs=[vmem] * len(row_counts),
        out_shape=[pltpu.VMEM((count, tokens), jnp.bfloat16) for count in row_counts],
        scratch_shapes=[order, order],
        compiler_params=with_vmem(4 + 6 * tokens * 256 // 2**20),
        cost_estimate=pl.CostEstimate(
            flops=0, bytes_accessed=4 * tokens * rows, transcendentals=0
        ),
        name="unpack",
    )(place, *pieces)


def join_kernel(*refs):
    pass


def join(arrays, after=()):
    count = len(arrays)
    hbm = pl.BlockSpec(memory_space=pl.ANY)
    return pl.pallas_call(
        join_kernel,
        in_specs=[hbm] * (count + len(after)),
        out_specs=[hbm] * count,
        out_shape=[jax.ShapeDtypeStruct(array.shape, array.dtype) for array in arrays],
        input_output_aliases={at: at for at in range(count)},
        compiler_params=with_vmem(1),
        name="join",
    )(*arrays, *after)


def preload_kernel(*refs):
    count = (len(refs) - 3) // 2
    token, sems = refs[-2:]
    outputs = refs[count + 1 :]
    copies = [pltpu.make_async_copy(refs[at], outputs[at], sems.at[at]) for at in range(count)]
    token[...] = jnp.zeros_like(token)
    for copy in copies:
        copy.start()
    for copy in copies:
        copy.wait()


def preload(arrays, after):
    return pl.pallas_call(
        preload_kernel,
        in_specs=[pl.BlockSpec(memory_space=pl.ANY)] * (len(arrays) + 1),
        out_specs=[pl.BlockSpec(memory_space=pltpu.VMEM)] * (len(arrays) + 1),
        out_shape=[pltpu.VMEM(array.shape, array.dtype) for array in arrays]
        + [jax.ShapeDtypeStruct((8, 128), jnp.float32)],
        scratch_shapes=[pltpu.SemaphoreType.DMA((len(arrays),))],
        compiler_params=with_vmem(4),
        cost_estimate=pl.CostEstimate(
            flops=0, bytes_accessed=sum(2 * array.size for array in arrays), transcendentals=0
        ),
        name="preload",
    )(*(pltpu.with_memory_space_constraint(array, pltpu.HBM) for array in arrays), after)


def write_back(buffers, outputs, sems, slot, rows, columns):
    return [
        pltpu.make_async_copy(
            buffer.at[slot, : rows.size, : columns.size],
            out.at[rows, columns],
            sems.at[slot, which],
        )
        for which, (buffer, out) in enumerate(zip(buffers, outputs))
    ]


def over_blocks(count, body):
    if count == 1:
        body(0)
    else:
        pl.loop(0, count)(body)


def update_tile(grad, weight, moment, second):
    first = beta_one * moment.astype(jnp.float32) + (1.0 - beta_one) * grad
    square = beta_two * second.astype(jnp.float32) + (1.0 - beta_two) * grad * grad
    inverse = lax.rsqrt(square)
    root = square * inverse + eps_adam
    inverse = inverse * (2.0 - root * inverse)
    return first, square, weight.astype(jnp.float32) - rate * first * inverse


def adam_kernel(strip, count_x, cuts, *refs):
    refs = list(refs)
    take = lambda count: [refs.pop(0) for _ in range(count)]
    x_refs = take(count_x)
    ins = [(take(len(cut)), *take(3)) for cut in cuts]
    power_ref = refs.pop(0)
    outs = [take(4) for _ in cuts]
    grads, buffers, power_sum, sems = (refs[0], refs[1]), (refs[2], refs[3]), refs[4], refs[5]
    pairs = x_refs[0].shape[1] // (2 * strip)
    base = 0
    for cut, (c_refs, w_ref, m_ref, v_ref), (hi_ref, lo_ref, *moments) in zip(cuts, ins, outs):
        for c_ref, low, rows in cut_rows(c_refs, cut):
            place = pl.ds(low, rows)

            def columns_of(pair, side):
                return pl.ds(pl.multiple_of((2 * pair + side) * strip, strip), strip)

            def multiply(pair, side, c_ref=c_ref, rows=rows):
                columns = columns_of(pair, side)
                rhs = jnp.concatenate([x_ref[:, columns] for x_ref in x_refs], axis=0)
                grads[side][:rows] = jnp.dot(c_ref[...], rhs, preferred_element_type=jnp.float32)

            def one_pair(pair, low=low, rows=rows, place=place, multiply=multiply):
                for side in range(2):
                    if side == 0:
                        multiply(pair, 1)
                    elif pairs > 1:
                        multiply(jnp.minimum(pair + 1, pairs - 1), 0)
                    columns = columns_of(pair, side)
                    if pairs > 1:

                        @pl.when(pair > 0)
                        def _():
                            for copy in write_back(buffers, moments, sems, side, place, columns):
                                copy.wait()

                    for row in range(0, rows, 16):
                        inside = slice(row, row + 16)
                        tile = slice(low + row, low + row + 16)
                        first, square, step = update_tile(
                            grads[side][inside],
                            w_ref[tile, columns],
                            m_ref[tile, columns],
                            v_ref[tile, columns],
                        )
                        buffers[0][side, inside] = first.astype(jnp.bfloat16)
                        buffers[1][side, inside] = square.astype(jnp.bfloat16)
                        hi = step.astype(jnp.bfloat16)
                        hi_ref[tile, columns] = hi
                        lo_ref[tile, columns] = (step - hi.astype(jnp.float32)).astype(
                            jnp.bfloat16
                        )
                        power = power_sum[inside]
                        for lane in range(0, strip, 128):
                            power += step[:, lane : lane + 128] * step[:, lane : lane + 128]
                        power_sum[inside] = power
                    for copy in write_back(buffers, moments, sems, side, place, columns):
                        copy.start()

            power_sum[:rows] = jnp.zeros((rows, 128), jnp.float32)
            multiply(0, 0)
            over_blocks(pairs, one_pair)
            start = base + low
            power_ref[:, start : start + rows] = jnp.sum(
                power_sum[:rows].T, axis=0, keepdims=True
            )
            for side in range(2):
                for copy in write_back(buffers, moments, sems, side, place, columns_of(0, side)):
                    copy.wait()
        base += sum(cut)


def cut_rows(c_refs, cut, largest=896):
    start = 0
    for c_ref, rows in zip(c_refs, cut):
        block = row_block(rows, largest)
        for low in range(0, rows, block):
            yield c_ref.at[low : low + block], start + low, block
        start += rows


def strip_of(width, largest=256):
    for strip in range(largest, 0, -128):
        if width % (2 * strip) == 0:
            return strip


def adam_pass(x_pieces, cotangents, states):
    width = x_pieces[0].shape[1]
    tokens = cotangents[0][0].shape[1]
    strip = strip_of(width)
    cuts = [[piece.shape[0] for piece in pieces] for pieces in cotangents]
    rows = sum(sum(cut) for cut in cuts)
    block = max(row_block(count, 896) for cut in cuts for count in cut)
    args, aliases, outs = list(x_pieces), {}, []
    for pieces, state in zip(cotangents, states):
        args += pieces
        aliases[len(args)] = len(outs) + 1
        aliases[len(args) + 1] = len(outs) + 2
        args += state
        shape = state[0].shape
        outs += [pltpu.VMEM(shape, jnp.bfloat16)] * 2
        outs += [jax.ShapeDtypeStruct(shape, jnp.bfloat16)] * 2
    vmem = pl.BlockSpec(memory_space=pltpu.VMEM)
    hbm = pl.BlockSpec(memory_space=pl.ANY)
    done = pl.pallas_call(
        functools.partial(adam_kernel, strip, len(x_pieces), cuts),
        in_specs=[vmem] * len(args),
        out_specs=[vmem] + [vmem, vmem, hbm, hbm] * len(states),
        out_shape=[jax.ShapeDtypeStruct((1, rows), jnp.float32), *outs],
        input_output_aliases=aliases,
        scratch_shapes=[
            pltpu.VMEM((block, strip), jnp.float32),
            pltpu.VMEM((block, strip), jnp.float32),
            pltpu.VMEM((2, block, strip), jnp.bfloat16),
            pltpu.VMEM((2, block, strip), jnp.bfloat16),
            pltpu.VMEM((block, 128), jnp.float32),
            pltpu.SemaphoreType.DMA((2, 2)),
        ],
        compiler_params=with_vmem(8 + (18 * block + 4 * tokens) * strip // 2**20),
        cost_estimate=pl.CostEstimate(
            flops=2 * tokens * rows * width, bytes_accessed=4 * rows * width, transcendentals=0
        ),
        name="adam",
    )(*(pltpu.with_memory_space_constraint(array, pltpu.VMEM) for array in args))
    return done[0], [done[at : at + 4] for at in range(1, len(done), 4)]


def finish_kernel(count, whole_width, matrices, *refs):
    powers, refs = refs[:count], refs[count:]
    parts, outputs, (buffer, sems) = refs[: 2 * matrices], refs[2 * matrices : -2], refs[-2:]
    slots = buffer.shape[0]
    base = 0
    for which, out_ref in enumerate(outputs):
        hi_ref, lo_ref = parts[2 * which : 2 * which + 2]
        rows, width = hi_ref.shape
        block = row_block(rows, 128)
        total = rows // block
        every = pl.ds(0, width)

        def one_block(at, base=base, block=block, total=total, every=every):
            slot = at % slots
            place = pl.ds(at * block, block)
            if total > slots:

                @pl.when(at >= slots)
                def _():
                    for copy in write_back([buffer], [out_ref], sems, slot, place, every):
                        copy.wait()

            lanes = pl.ds(base + at * block, block)
            power = powers[0][:, lanes]
            for other in powers[1:]:
                power = power + other[:, lanes]
            scale = 1.0 / jnp.sqrt(power / whole_width + eps_norm)
            scale = jnp.broadcast_to(scale, (128, block)).T
            for row in range(0, block, 16):
                inside = slice(row, row + 16)
                tile = pl.ds(at * block + row, 16)
                for lane in range(0, width, 128):
                    columns = slice(lane, lane + 128)
                    step = hi_ref[tile, columns].astype(jnp.float32)
                    step = step + lo_ref[tile, columns].astype(jnp.float32)
                    buffer[slot, inside, columns] = (step * scale[inside]).astype(jnp.bfloat16)
            for copy in write_back([buffer], [out_ref], sems, slot, place, every):
                copy.start()

        over_blocks(total, one_block)
        for at in range(max(0, total - slots), total):
            place = pl.ds(at * block, block)
            for copy in write_back([buffer], [out_ref], sems, at % slots, place, every):
                copy.wait()
        base += rows


def finish_rows(parts, powers, whole_width):
    shapes = [array.shape for array in parts[::2]]
    width = shapes[0][1]
    block = max(row_block(shape[0], 128) for shape in shapes)
    vmem = pl.BlockSpec(memory_space=pltpu.VMEM)
    return pl.pallas_call(
        functools.partial(finish_kernel, len(powers), whole_width, len(shapes)),
        in_specs=[vmem] * (len(powers) + len(parts)),
        out_specs=[pl.BlockSpec(memory_space=pl.ANY)] * len(shapes),
        out_shape=[jax.ShapeDtypeStruct(shape, jnp.bfloat16) for shape in shapes],
        scratch_shapes=[
            pltpu.VMEM((4, block, width), jnp.bfloat16),
            pltpu.SemaphoreType.DMA((4, 1)),
        ],
        compiler_params=with_vmem(8),
        cost_estimate=pl.CostEstimate(
            flops=sum(2 * rows * width for rows, _ in shapes),
            bytes_accessed=sum(2 * rows * width for rows, _ in shapes),
            transcendentals=0,
        ),
        name="finish",
    )(*powers, *(pltpu.with_memory_space_constraint(array, pltpu.VMEM) for array in parts))


def swap(array, axis, bit):
    return lax.ppermute(array, axis, [(at, at ^ bit) for at in range(lax.axis_size(axis))])


def from_others(pair, axis):
    bit = lax.axis_size(axis) // 2
    got = {0: pair[0], bit: pair[1]}
    while bit > 1:
        bit //= 2
        for turn in list(got):
            got[turn ^ bit] = swap(got[turn], axis, bit)
    return [got[turn] for turn in range(len(got))]


def straight_from_others(array, axis):
    size = lax.axis_size(axis)
    return [array] + [
        lax.ppermute(array, axis, [(at, at ^ turn) for at in range(size)])
        for turn in range(1, size)
    ]


def per_device(
    layer_input,
    query_cotangent,
    key_cotangent,
    up_cotangent,
    query_weight,
    key_weight,
    up_weight,
    moment_query,
    moment_key,
    moment_up,
    second_query,
    second_key,
    second_up,
):
    groups = lax.axis_size("dp")
    cols = lax.axis_size("col")
    part = layer_input.shape[0] // cols
    whole_width = layer_input.shape[1] * cols
    states = (
        (query_weight, moment_query, second_query),
        (key_weight, moment_key, second_key),
        (up_weight, moment_up, second_up),
    )
    place = jnp.stack([lax.axis_index("col"), lax.axis_index("dp")]).astype(jnp.int32)
    plan = chunk_plan([state[0].shape[0] for state in states])
    packed = [*pack((query_cotangent, key_cotangent, up_cotangent), plan, groups, part, place)]
    behind, ahead = [layer_input], [layer_input]
    swaps = [[], []]
    for chunk in range(2):
        one, two = ring_step(behind[-1], ahead[-1], "dp")
        owned = lax.all_to_all(packed[chunk], "dp", split_axis=0, concat_axis=0, tiled=True)
        if chunk == 0:
            owned, one, two, packed[1] = join((owned, one, two, packed[1]))
            swaps[0] = [owned, swap(owned, "col", cols // 2)]
        else:
            owned, one, two, swaps[0][1] = join((owned, one, two, swaps[0][1]))
            swaps[1] = [owned, swap(owned, "col", cols // 2)]
        behind.append(one)
        ahead.append(two)
    *held, loaded = preload([array for state in states for array in state], owned)
    held = [held[at : at + 3] for at in range(0, len(held), 3)]
    middle = []
    while 2 * len(behind) <= groups:
        if 2 * len(behind) < groups:
            one, two = ring_step(behind[-1], ahead[-1], "dp")
            if loaded is not None:
                one, two, swaps[1][1] = join((one, two, swaps[1][1]), (loaded,))
                loaded = None
            behind.append(one)
            ahead.append(two)
        else:
            middle = list(ring_step(*halves(behind[-1], ahead[-1]), "dp"))
            break
    x_pieces = [layer_input, *ahead[1:], *middle, *behind[:0:-1]]
    cotangents = [[], [], []]
    for got, pieces in zip(swaps, plan):
        every = unpack(
            from_others(got, "col"), [high - low for _, low, high in pieces], place
        )
        for (which, _, _), cotangent in zip(pieces, every):
            cotangents[which].append(cotangent)
    updated = [None] * 3
    moments = [None] * 3
    passes = []
    for group in ((2,), (0, 1)):
        power, made = adam_pass(
            x_pieces, [cotangents[which] for which in group], [held[which] for which in group]
        )
        passes.append((group, straight_from_others(power, "col"), made))
    for group, powers, made in passes:
        parts = [array for done in made for array in done[:2]]
        for which, done, array in zip(group, made, finish_rows(parts, powers, whole_width)):
            updated[which] = array
            moments[which] = done[2:]
    return (*updated, *(done[0] for done in moments), *(done[1] for done in moments))


def solution(mesh):
    tokens_split = P("dp", None)
    split = P("dp", "col")
    return jax.shard_map(
        per_device,
        mesh=mesh,
        in_specs=(split, *(tokens_split,) * 3, *(split,) * 9),
        out_specs=(split,) * 9,
        check_vma=False,
    )
```

```python
import functools

import jax
import jax.numpy as jnp
from jax import lax
from jax.experimental import pallas as pl
from jax.experimental.pallas import tpu as pltpu
from jax.sharding import PartitionSpec as P

beta_one = 0.9
beta_two = 0.95
rate = 0.1
eps_adam = 1e-08
eps_norm = 1e-06


def with_vmem(mebibytes):
    return pltpu.CompilerParams(vmem_limit_bytes=mebibytes * 1024 * 1024)


def row_block(rows, largest=256):
    for block in range(largest, 0, -128):
        if rows % block == 0:
            return block
    return rows


def ring_order(groups):
    return [*range(0, groups, 2), *range(groups - 1 - groups % 2, 0, -2)]


def ring_place(at, groups):
    return jnp.where(at % 2 == 0, at // 2, groups - 1 - at // 2)


def pack_kernel(plan, groups, at_ref, *refs):
    inputs, outputs = refs[: -len(plan)], refs[-len(plan) :]
    for pieces, out_ref in zip(plan, outputs):
        start = 0
        for which, low, high in pieces:
            ref = inputs[which]
            rows = ref.shape[1] // groups
            for group in range(groups):
                out_ref[group, :, start : start + high - low] = ref[
                    :, group * rows + low : group * rows + high
                ]
            start += high - low


def pack(cotangents, plan, groups, part, place):
    outs = [
        jax.ShapeDtypeStruct(
            (groups, part, sum(high - low for _, low, high in pieces)), jnp.bfloat16
        )
        for pieces in plan
    ]
    return pl.pallas_call(
        functools.partial(pack_kernel, plan, groups),
        grid_spec=pltpu.PrefetchScalarGridSpec(
            num_scalar_prefetch=1,
            grid=(1,),
            in_specs=[
                pl.BlockSpec((part, array.shape[1]), lambda i, at: (at[0], 0))
                for array in cotangents
            ],
            out_specs=[pl.BlockSpec(out.shape, lambda i, at: (0, 0, 0)) for out in outs],
        ),
        out_shape=outs,
        compiler_params=with_vmem(16),
        cost_estimate=pl.CostEstimate(
            flops=0,
            bytes_accessed=4 * part * sum(array.shape[1] for array in cotangents),
            transcendentals=0,
        ),
        name="pack",
    )(place, *(pltpu.with_memory_space_constraint(array, pltpu.HBM) for array in cotangents))


def halves_kernel(one_ref, two_ref, first_ref, last_ref):
    half = first_ref.shape[0]
    first_ref[...] = one_ref[:half]
    last_ref[...] = two_ref[half:]


def halves(one, two):
    half = jax.ShapeDtypeStruct((one.shape[0] // 2, one.shape[1]), one.dtype)
    vmem = pl.BlockSpec(memory_space=pltpu.VMEM)
    return pl.pallas_call(
        halves_kernel,
        in_specs=[vmem] * 2,
        out_specs=[vmem] * 2,
        out_shape=[half] * 2,
        compiler_params=with_vmem(4),
        cost_estimate=pl.CostEstimate(
            flops=0, bytes_accessed=4 * one.size, transcendentals=0
        ),
        name="halves",
    )(one, two)


def ring_paths(groups):
    order = ring_order(groups)
    onward = list(zip(order, order[1:] + order[:1]))
    return onward, [(to, at) for at, to in onward]


def ring_step(one, two, axis):
    onward, back = ring_paths(lax.axis_size(axis))
    return lax.ppermute(one, axis, onward), lax.ppermute(two, axis, back)


def unpack_kernel(count, at_ref, *refs):
    pieces, outputs, orders = refs[:count], refs[count:-2], refs[-2:]
    groups = pieces[0].shape[0]
    here = ring_place(at_ref[1], groups)
    slots = [(ring_place(group, groups) - here + groups) % groups for group in range(groups)]
    low = 0
    for out_ref in outputs:
        rows = out_ref.shape[0]
        for start in range(0, rows, 128):
            high = min(start + 128, rows)
            order = orders[start // 128 % 2]
            for group, slot in enumerate(slots):
                for turn, piece in enumerate(pieces):
                    order[slot * count + (at_ref[0] ^ turn), :, : high - start] = piece[
                        group, :, low + start : low + high
                    ]
            out_ref[start:high] = order[...].reshape(-1, 128).T[: high - start]
        low += rows


def unpack(pieces, row_counts, place):
    groups, part, rows = pieces[0].shape
    tokens = groups * part * len(pieces)
    vmem = pl.BlockSpec(memory_space=pltpu.VMEM)
    order = pltpu.VMEM((groups * len(pieces), part, 128), jnp.bfloat16)
    return pl.pallas_call(
        functools.partial(unpack_kernel, len(pieces)),
        in_specs=[pl.BlockSpec(memory_space=pltpu.SMEM)] + [vmem] * len(pieces),
        out_specs=[vmem] * len(row_counts),
        out_shape=[pltpu.VMEM((count, tokens), jnp.bfloat16) for count in row_counts],
        scratch_shapes=[order, order],
        compiler_params=with_vmem(4 + 6 * tokens * 256 // 2**20),
        cost_estimate=pl.CostEstimate(
            flops=0, bytes_accessed=4 * tokens * rows, transcendentals=0
        ),
        name="unpack",
    )(place, *pieces)


def join_kernel(*refs):
    pass


def join(arrays, after=()):
    count = len(arrays)
    hbm = pl.BlockSpec(memory_space=pl.ANY)
    return pl.pallas_call(
        join_kernel,
        in_specs=[hbm] * (count + len(after)),
        out_specs=[hbm] * count,
        out_shape=[jax.ShapeDtypeStruct(array.shape, array.dtype) for array in arrays],
        input_output_aliases={at: at for at in range(count)},
        compiler_params=with_vmem(1),
        name="join",
    )(*arrays, *after)


def preload_kernel(*refs):
    count = (len(refs) - 3) // 2
    token, sems = refs[-2:]
    outputs = refs[count + 1 :]
    copies = [pltpu.make_async_copy(refs[at], outputs[at], sems.at[at]) for at in range(count)]
    token[...] = jnp.zeros_like(token)
    for copy in copies:
        copy.start()
    for copy in copies:
        copy.wait()


def preload(arrays, after):
    return pl.pallas_call(
        preload_kernel,
        in_specs=[pl.BlockSpec(memory_space=pl.ANY)] * (len(arrays) + 1),
        out_specs=[pl.BlockSpec(memory_space=pltpu.VMEM)] * (len(arrays) + 1),
        out_shape=[pltpu.VMEM(array.shape, array.dtype) for array in arrays]
        + [jax.ShapeDtypeStruct((8, 128), jnp.float32)],
        scratch_shapes=[pltpu.SemaphoreType.DMA((len(arrays),))],
        compiler_params=with_vmem(4),
        cost_estimate=pl.CostEstimate(
            flops=0, bytes_accessed=sum(2 * array.size for array in arrays), transcendentals=0
        ),
        name="preload",
    )(*(pltpu.with_memory_space_constraint(array, pltpu.HBM) for array in arrays), after)


def write_back(buffers, outputs, sems, slot, at):
    return [
        pltpu.make_async_copy(buffer.at[slot, : at.size], out.at[at], sems.at[slot, which])
        for which, (buffer, out) in enumerate(zip(buffers, outputs))
    ]


def over_blocks(count, body):
    if count == 1:
        body(0)
    else:
        pl.loop(0, count)(body)


def update_tile(grad, weight, moment, second):
    first = beta_one * moment.astype(jnp.float32) + (1.0 - beta_one) * grad
    square = beta_two * second.astype(jnp.float32) + (1.0 - beta_two) * grad * grad
    inverse = lax.rsqrt(square)
    root = square * inverse + eps_adam
    inverse = inverse * (2.0 - root * inverse)
    return first, square, weight.astype(jnp.float32) - rate * first * inverse


def adam_kernel(strip, count_x, cuts, *refs):
    refs = list(refs)
    take = lambda count: [refs.pop(0) for _ in range(count)]
    x_refs = take(count_x)
    ins = [(take(len(cut)), *take(3)) for cut in cuts]
    power_ref = refs.pop(0)
    outs = [take(4) for _ in cuts]
    grads, buffers, power_sum, sems = (refs[0], refs[1]), (refs[2], refs[3]), refs[4], refs[5]
    width = x_refs[0].shape[1]
    strips = width // strip
    base = 0
    for cut, (c_refs, w_ref, m_ref, v_ref), (hi_ref, lo_ref, *moments) in zip(cuts, ins, outs):
        low = 0
        for c_ref, rows in zip(c_refs, cut):
            block = row_block(rows)
            count = rows // block

            def multiply(at, which, c_ref=c_ref, block=block):
                lhs = c_ref[pl.ds(at * block, block), :]
                columns = slice(which * strip, (which + 1) * strip)
                rhs = jnp.concatenate([x_ref[:, columns] for x_ref in x_refs], axis=0)
                grads[which % 2][:block] = jnp.dot(lhs, rhs, preferred_element_type=jnp.float32)

            def one_block(at, low=low, base=base, count=count, block=block, multiply=multiply):
                slot = at % 2
                place = pl.ds(low + at * block, block)
                if count > 2:

                    @pl.when(at >= 2)
                    def _():
                        for copy in write_back(buffers, moments, sems, slot, place):
                            copy.wait()

                for which in range(strips):
                    if which + 1 < strips:
                        multiply(at, which + 1)
                    elif count > 1:
                        multiply(jnp.minimum(at + 1, count - 1), 0)
                    columns = slice(which * strip, (which + 1) * strip)
                    for row in range(0, block, 16):
                        inside = slice(row, row + 16)
                        tile = pl.ds(low + at * block + row, 16)
                        first, square, step = update_tile(
                            grads[which % 2][inside],
                            w_ref[tile, columns],
                            m_ref[tile, columns],
                            v_ref[tile, columns],
                        )
                        buffers[0][slot, inside, columns] = first.astype(jnp.bfloat16)
                        buffers[1][slot, inside, columns] = square.astype(jnp.bfloat16)
                        hi = step.astype(jnp.bfloat16)
                        hi_ref[tile, columns] = hi
                        lo_ref[tile, columns] = (step - hi.astype(jnp.float32)).astype(
                            jnp.bfloat16
                        )
                        power = step[:, :128] * step[:, :128]
                        for lane in range(128, strip, 128):
                            power += step[:, lane : lane + 128] * step[:, lane : lane + 128]
                        if which:
                            power += power_sum[inside]
                        power_sum[inside] = power
                power_ref[:, pl.ds(base + low + at * block, block)] = jnp.sum(
                    power_sum[:block].T, axis=0, keepdims=True
                )
                for copy in write_back(buffers, moments, sems, slot, place):
                    copy.start()

            multiply(0, 0)
            over_blocks(count, one_block)
            for at in range(max(0, count - 2), count):
                place = pl.ds(low + at * block, block)
                for copy in write_back(buffers, moments, sems, at % 2, place):
                    copy.wait()
            low += rows
        base += low


def strip_of(width, largest=256):
    for strip in range(largest, 0, -128):
        if width % (2 * strip) == 0:
            return strip


def adam_pass(x_pieces, cotangents, states):
    width = x_pieces[0].shape[1]
    tokens = cotangents[0][0].shape[1]
    strip = strip_of(width)
    cuts = [[piece.shape[0] for piece in pieces] for pieces in cotangents]
    rows = sum(sum(cut) for cut in cuts)
    block = max(row_block(count) for cut in cuts for count in cut)
    args, aliases, outs = list(x_pieces), {}, []
    for pieces, state in zip(cotangents, states):
        args += pieces
        aliases[len(args)] = len(outs) + 1
        aliases[len(args) + 1] = len(outs) + 2
        args += state
        shape = state[0].shape
        outs += [pltpu.VMEM(shape, jnp.bfloat16)] * 2
        outs += [jax.ShapeDtypeStruct(shape, jnp.bfloat16)] * 2
    vmem = pl.BlockSpec(memory_space=pltpu.VMEM)
    hbm = pl.BlockSpec(memory_space=pl.ANY)
    done = pl.pallas_call(
        functools.partial(adam_kernel, strip, len(x_pieces), cuts),
        in_specs=[vmem] * len(args),
        out_specs=[vmem] + [vmem, vmem, hbm, hbm] * len(states),
        out_shape=[jax.ShapeDtypeStruct((1, rows), jnp.float32), *outs],
        input_output_aliases=aliases,
        scratch_shapes=[
            pltpu.VMEM((block, strip), jnp.float32),
            pltpu.VMEM((block, strip), jnp.float32),
            pltpu.VMEM((2, block, width), jnp.bfloat16),
            pltpu.VMEM((2, block, width), jnp.bfloat16),
            pltpu.VMEM((block, 128), jnp.float32),
            pltpu.SemaphoreType.DMA((2, 2)),
        ],
        compiler_params=with_vmem(12),
        cost_estimate=pl.CostEstimate(
            flops=2 * tokens * rows * width, bytes_accessed=4 * rows * width, transcendentals=0
        ),
        name="adam",
    )(*(pltpu.with_memory_space_constraint(array, pltpu.VMEM) for array in args))
    return done[0], [done[at : at + 4] for at in range(1, len(done), 4)]


def finish_kernel(count, whole_width, matrices, *refs):
    powers, refs = refs[:count], refs[count:]
    parts, outputs, (buffer, sems) = refs[: 2 * matrices], refs[-2 - matrices : -2], refs[-2:]
    slots = buffer.shape[0]
    base = 0
    for which, out_ref in enumerate(outputs):
        hi_ref, lo_ref = parts[2 * which : 2 * which + 2]
        rows, width = hi_ref.shape
        block = row_block(rows, 128)
        total = rows // block

        def one_block(at, base=base, block=block, total=total):
            slot = at % slots
            place = pl.ds(at * block, block)
            if total > slots:

                @pl.when(at >= slots)
                def _():
                    for copy in write_back([buffer], [out_ref], sems, slot, place):
                        copy.wait()

            lanes = pl.ds(base + at * block, block)
            power = powers[0][:, lanes]
            for other in powers[1:]:
                power = power + other[:, lanes]
            scale = 1.0 / jnp.sqrt(power / whole_width + eps_norm)
            scale = jnp.broadcast_to(scale, (128, block)).T
            for row in range(0, block, 16):
                inside = slice(row, row + 16)
                tile = pl.ds(at * block + row, 16)
                for lane in range(0, width, 128):
                    columns = slice(lane, lane + 128)
                    step = hi_ref[tile, columns].astype(jnp.float32)
                    step = step + lo_ref[tile, columns].astype(jnp.float32)
                    buffer[slot, inside, columns] = (step * scale[inside]).astype(jnp.bfloat16)
            for copy in write_back([buffer], [out_ref], sems, slot, place):
                copy.start()

        over_blocks(total, one_block)
        for at in range(max(0, total - slots), total):
            place = pl.ds(at * block, block)
            for copy in write_back([buffer], [out_ref], sems, at % slots, place):
                copy.wait()
        base += rows


def finish_rows(parts, powers, whole_width, after):
    shapes = [array.shape for array in parts[::2]]
    width = shapes[0][1]
    block = max(row_block(shape[0], 128) for shape in shapes)
    vmem = pl.BlockSpec(memory_space=pltpu.VMEM)
    return pl.pallas_call(
        functools.partial(finish_kernel, len(powers), whole_width, len(shapes)),
        in_specs=[vmem] * (len(powers) + len(parts))
        + [pl.BlockSpec(memory_space=pl.ANY)] * len(after),
        out_specs=[pl.BlockSpec(memory_space=pl.ANY)] * len(shapes),
        out_shape=[jax.ShapeDtypeStruct(shape, jnp.bfloat16) for shape in shapes],
        scratch_shapes=[
            pltpu.VMEM((4, block, width), jnp.bfloat16),
            pltpu.SemaphoreType.DMA((4, 1)),
        ],
        compiler_params=with_vmem(8),
        cost_estimate=pl.CostEstimate(
            flops=sum(2 * rows * width for rows, _ in shapes),
            bytes_accessed=sum(2 * rows * width for rows, _ in shapes),
            transcendentals=0,
        ),
        name="finish",
    )(
        *powers,
        *(pltpu.with_memory_space_constraint(array, pltpu.VMEM) for array in parts),
        *after,
    )


def swap(array, axis, bit):
    return lax.ppermute(array, axis, [(at, at ^ bit) for at in range(lax.axis_size(axis))])


def from_others(pair, axis):
    bit = lax.axis_size(axis) // 2
    got = {0: pair[0], bit: pair[1]}
    while bit > 1:
        bit //= 2
        for turn in list(got):
            got[turn ^ bit] = swap(got[turn], axis, bit)
    return [got[turn] for turn in range(len(got))]


def straight_from_others(array, axis):
    size = lax.axis_size(axis)
    return [array] + [
        lax.ppermute(array, axis, [(at, at ^ turn) for at in range(size)])
        for turn in range(1, size)
    ]


def per_device(
    layer_input,
    query_cotangent,
    key_cotangent,
    up_cotangent,
    query_weight,
    key_weight,
    up_weight,
    moment_query,
    moment_key,
    moment_up,
    second_query,
    second_key,
    second_up,
):
    groups = lax.axis_size("dp")
    cols = lax.axis_size("col")
    part = layer_input.shape[0] // cols
    whole_width = layer_input.shape[1] * cols
    states = (
        (query_weight, moment_query, second_query),
        (key_weight, moment_key, second_key),
        (up_weight, moment_up, second_up),
    )
    place = jnp.stack([lax.axis_index("col"), lax.axis_index("dp")]).astype(jnp.int32)
    plan = [[(2, 0, up_weight.shape[0])]]
    plan.append([(which, 0, states[which][0].shape[0]) for which in (0, 1)])
    packed = pack((query_cotangent, key_cotangent, up_cotangent), plan, groups, part, place)
    one, two = ring_step(layer_input, layer_input, "dp")
    chunk, one, two = join((packed[0], one, two))
    behind, ahead = [layer_input, one], [layer_input, two]
    owned = lax.all_to_all(chunk, "dp", split_axis=0, concat_axis=0, tiled=True)
    one, two = ring_step(one, two, "dp")
    owned, one, two, chunk = join((owned, one, two, packed[1]))
    behind.append(one)
    ahead.append(two)
    swaps = [(owned, swap(owned, "col", cols // 2))]
    owned = lax.all_to_all(chunk, "dp", split_axis=0, concat_axis=0, tiled=True)
    one, two = ring_step(one, two, "dp")
    owned, one, two = join((owned, one, two), (swaps[0][1],))
    behind.append(one)
    ahead.append(two)
    swaps.append((owned, swap(owned, "col", cols // 2)))
    *held, _ = preload([array for state in states for array in state], owned)
    held = [held[at : at + 3] for at in range(0, len(held), 3)]
    while 2 * len(behind) < groups:
        one, two = ring_step(one, two, "dp")
        behind.append(one)
        ahead.append(two)
    middle = ring_step(*halves(one, two), "dp")
    x_pieces = [layer_input, *ahead[1:], *middle, *behind[:0:-1]]
    cotangents = [[], [], []]
    for got, pieces in zip(swaps, plan):
        every = unpack(
            from_others(got, "col"), [high - low for _, low, high in pieces], place
        )
        for (which, _, _), cotangent in zip(pieces, every):
            cotangents[which].append(cotangent)
    updated = [None] * 3
    moments = [None] * 3
    passes = []
    for group in ((2,), (0, 1)):
        power, made = adam_pass(
            x_pieces, [cotangents[which] for which in group], [held[which] for which in group]
        )
        passes.append((group, straight_from_others(power, "col"), made))
    for group, powers, made in passes:
        parts = [array for done in made for array in done[:2]]
        after = [array for array in updated if array is not None]
        finished = finish_rows(parts, powers, whole_width, after)
        for which, done, array in zip(group, made, finished):
            updated[which] = array
            moments[which] = done[2:]
    return (*updated, *(done[0] for done in moments), *(done[1] for done in moments))


def solution(mesh):
    tokens_split = P("dp", None)
    split = P("dp", "col")
    return jax.shard_map(
        per_device,
        mesh=mesh,
        in_specs=(split, *(tokens_split,) * 3, *(split,) * 9),
        out_specs=(split,) * 9,
        check_vma=False,
    )
```

```python
import functools

import jax
import jax.numpy as jnp
from jax import lax
from jax.experimental import pallas as pl
from jax.experimental.pallas import tpu as pltpu
from jax.sharding import PartitionSpec as P

beta_one = 0.9
beta_two = 0.95
rate = 0.1
eps_adam = 1e-08
eps_norm = 1e-06


def with_vmem(mebibytes):
    return pltpu.CompilerParams(vmem_limit_bytes=mebibytes * 1024 * 1024)


def row_block(rows, largest=256):
    for block in range(largest, 0, -128):
        if rows % block == 0:
            return block
    return rows


def ring_order(groups):
    return [*range(0, groups, 2), *range(groups - 1 - groups % 2, 0, -2)]


def ring_place(at, groups):
    return jnp.where(at % 2 == 0, at // 2, groups - 1 - at // 2)


def pack_kernel(plan, groups, at_ref, *refs):
    inputs, outputs = refs[: -len(plan)], refs[-len(plan) :]
    for pieces, out_ref in zip(plan, outputs):
        start = 0
        for which, low, high in pieces:
            ref = inputs[which]
            rows = ref.shape[1] // groups
            for group in range(groups):
                out_ref[group, :, start : start + high - low] = ref[
                    :, group * rows + low : group * rows + high
                ]
            start += high - low


def pack(cotangents, plan, groups, part, place):
    outs = [
        jax.ShapeDtypeStruct(
            (groups, part, sum(high - low for _, low, high in pieces)), jnp.bfloat16
        )
        for pieces in plan
    ]
    return pl.pallas_call(
        functools.partial(pack_kernel, plan, groups),
        grid_spec=pltpu.PrefetchScalarGridSpec(
            num_scalar_prefetch=1,
            grid=(1,),
            in_specs=[
                pl.BlockSpec((part, array.shape[1]), lambda i, at: (at[0], 0))
                for array in cotangents
            ],
            out_specs=[pl.BlockSpec(out.shape, lambda i, at: (0, 0, 0)) for out in outs],
        ),
        out_shape=outs,
        compiler_params=with_vmem(16),
        cost_estimate=pl.CostEstimate(
            flops=0,
            bytes_accessed=4 * part * sum(array.shape[1] for array in cotangents),
            transcendentals=0,
        ),
        name="pack",
    )(place, *(pltpu.with_memory_space_constraint(array, pltpu.HBM) for array in cotangents))


def halves_kernel(one_ref, two_ref, first_ref, last_ref):
    half = first_ref.shape[0]
    first_ref[...] = one_ref[:half]
    last_ref[...] = two_ref[half:]


def halves(one, two):
    half = jax.ShapeDtypeStruct((one.shape[0] // 2, one.shape[1]), one.dtype)
    vmem = pl.BlockSpec(memory_space=pltpu.VMEM)
    return pl.pallas_call(
        halves_kernel,
        in_specs=[vmem] * 2,
        out_specs=[vmem] * 2,
        out_shape=[half] * 2,
        compiler_params=with_vmem(4),
        cost_estimate=pl.CostEstimate(
            flops=0, bytes_accessed=4 * one.size, transcendentals=0
        ),
        name="halves",
    )(one, two)


def ring_paths(groups):
    order = ring_order(groups)
    onward = list(zip(order, order[1:] + order[:1]))
    return onward, [(to, at) for at, to in onward]


def ring_step(one, two, axis):
    onward, back = ring_paths(lax.axis_size(axis))
    return lax.ppermute(one, axis, onward), lax.ppermute(two, axis, back)


def unpack_kernel(count, at_ref, *refs):
    pieces, outputs, orders = refs[:count], refs[count:-2], refs[-2:]
    groups = pieces[0].shape[0]
    here = ring_place(at_ref[1], groups)
    slots = [(ring_place(group, groups) - here + groups) % groups for group in range(groups)]
    low = 0
    for out_ref in outputs:
        rows = out_ref.shape[0]
        for start in range(0, rows, 128):
            high = min(start + 128, rows)
            order = orders[start // 128 % 2]
            for group, slot in enumerate(slots):
                for turn, piece in enumerate(pieces):
                    order[slot * count + (at_ref[0] ^ turn), :, : high - start] = piece[
                        group, :, low + start : low + high
                    ]
            out_ref[start:high] = order[...].reshape(-1, 128).T[: high - start]
        low += rows


def unpack(pieces, row_counts, place):
    groups, part, rows = pieces[0].shape
    tokens = groups * part * len(pieces)
    vmem = pl.BlockSpec(memory_space=pltpu.VMEM)
    order = pltpu.VMEM((groups * len(pieces), part, 128), jnp.bfloat16)
    return pl.pallas_call(
        functools.partial(unpack_kernel, len(pieces)),
        in_specs=[pl.BlockSpec(memory_space=pltpu.SMEM)] + [vmem] * len(pieces),
        out_specs=[vmem] * len(row_counts),
        out_shape=[pltpu.VMEM((count, tokens), jnp.bfloat16) for count in row_counts],
        scratch_shapes=[order, order],
        compiler_params=with_vmem(4 + 6 * tokens * 256 // 2**20),
        cost_estimate=pl.CostEstimate(
            flops=0, bytes_accessed=4 * tokens * rows, transcendentals=0
        ),
        name="unpack",
    )(place, *pieces)


def join_kernel(*refs):
    pass


def join(arrays, after=()):
    count = len(arrays)
    hbm = pl.BlockSpec(memory_space=pl.ANY)
    return pl.pallas_call(
        join_kernel,
        in_specs=[hbm] * (count + len(after)),
        out_specs=[hbm] * count,
        out_shape=[jax.ShapeDtypeStruct(array.shape, array.dtype) for array in arrays],
        input_output_aliases={at: at for at in range(count)},
        compiler_params=with_vmem(1),
        name="join",
    )(*arrays, *after)


def preload_kernel(*refs):
    count = (len(refs) - 3) // 2
    token, sems = refs[-2:]
    outputs = refs[count + 1 :]
    copies = [pltpu.make_async_copy(refs[at], outputs[at], sems.at[at]) for at in range(count)]
    token[...] = jnp.zeros_like(token)
    for copy in copies:
        copy.start()
    for copy in copies:
        copy.wait()


def preload(arrays, after):
    return pl.pallas_call(
        preload_kernel,
        in_specs=[pl.BlockSpec(memory_space=pl.ANY)] * (len(arrays) + 1),
        out_specs=[pl.BlockSpec(memory_space=pltpu.VMEM)] * (len(arrays) + 1),
        out_shape=[pltpu.VMEM(array.shape, array.dtype) for array in arrays]
        + [jax.ShapeDtypeStruct((8, 128), jnp.float32)],
        scratch_shapes=[pltpu.SemaphoreType.DMA((len(arrays),))],
        compiler_params=with_vmem(4),
        cost_estimate=pl.CostEstimate(
            flops=0, bytes_accessed=sum(2 * array.size for array in arrays), transcendentals=0
        ),
        name="preload",
    )(*(pltpu.with_memory_space_constraint(array, pltpu.HBM) for array in arrays), after)


def write_back(buffers, outputs, sems, slot, at):
    return [
        pltpu.make_async_copy(buffer.at[slot, : at.size], out.at[at], sems.at[slot, which])
        for which, (buffer, out) in enumerate(zip(buffers, outputs))
    ]


def over_blocks(count, body):
    if count == 1:
        body(0)
    else:
        pl.loop(0, count)(body)


def update_tile(grad, weight, moment, second):
    first = beta_one * moment.astype(jnp.float32) + (1.0 - beta_one) * grad
    square = beta_two * second.astype(jnp.float32) + (1.0 - beta_two) * grad * grad
    inverse = lax.rsqrt(square)
    root = square * inverse + eps_adam
    inverse = inverse * (2.0 - root * inverse)
    return first, square, weight.astype(jnp.float32) - rate * first * inverse


def adam_kernel(strip, count_x, cuts, *refs):
    refs = list(refs)
    take = lambda count: [refs.pop(0) for _ in range(count)]
    x_refs = take(count_x)
    ins = [(take(len(cut)), *take(3)) for cut in cuts]
    power_ref = refs.pop(0)
    outs = [take(4) for _ in cuts]
    grads, buffers, power_sum, sems = (refs[0], refs[1]), (refs[2], refs[3]), refs[4], refs[5]
    width = x_refs[0].shape[1]
    strips = width // strip
    base = 0
    for cut, (c_refs, w_ref, m_ref, v_ref), (hi_ref, lo_ref, *moments) in zip(cuts, ins, outs):
        low = 0
        for c_ref, rows in zip(c_refs, cut):
            block = row_block(rows, 128)
            count = rows // block

            def multiply(at, which, c_ref=c_ref, block=block):
                lhs = c_ref[pl.ds(at * block, block), :]
                columns = slice(which * strip, (which + 1) * strip)
                rhs = jnp.concatenate([x_ref[:, columns] for x_ref in x_refs], axis=0)
                grads[which % 2][:block] = jnp.dot(lhs, rhs, preferred_element_type=jnp.float32)

            def one_block(at, low=low, base=base, count=count, block=block, multiply=multiply):
                slot = at % 2
                place = pl.ds(low + at * block, block)
                if count > 2:

                    @pl.when(at >= 2)
                    def _():
                        for copy in write_back(buffers, moments, sems, slot, place):
                            copy.wait()

                for which in range(strips):
                    if which + 1 < strips:
                        multiply(at, which + 1)
                    elif count > 1:
                        multiply(jnp.minimum(at + 1, count - 1), 0)
                    columns = slice(which * strip, (which + 1) * strip)
                    for row in range(0, block, 16):
                        inside = slice(row, row + 16)
                        tile = pl.ds(low + at * block + row, 16)
                        first, square, step = update_tile(
                            grads[which % 2][inside],
                            w_ref[tile, columns],
                            m_ref[tile, columns],
                            v_ref[tile, columns],
                        )
                        buffers[0][slot, inside, columns] = first.astype(jnp.bfloat16)
                        buffers[1][slot, inside, columns] = square.astype(jnp.bfloat16)
                        hi = step.astype(jnp.bfloat16)
                        hi_ref[tile, columns] = hi
                        lo_ref[tile, columns] = (step - hi.astype(jnp.float32)).astype(
                            jnp.bfloat16
                        )
                        power = step[:, :128] * step[:, :128]
                        for lane in range(128, strip, 128):
                            power += step[:, lane : lane + 128] * step[:, lane : lane + 128]
                        if which:
                            power += power_sum[inside]
                        power_sum[inside] = power
                power_ref[:, pl.ds(base + low + at * block, block)] = jnp.sum(
                    power_sum[:block].T, axis=0, keepdims=True
                )
                for copy in write_back(buffers, moments, sems, slot, place):
                    copy.start()

            multiply(0, 0)
            over_blocks(count, one_block)
            for at in range(max(0, count - 2), count):
                place = pl.ds(low + at * block, block)
                for copy in write_back(buffers, moments, sems, at % 2, place):
                    copy.wait()
            low += rows
        base += low


def strip_of(width, largest=256):
    for strip in range(largest, 0, -128):
        if width % (2 * strip) == 0:
            return strip


def adam_pass(x_pieces, cotangents, states):
    width = x_pieces[0].shape[1]
    tokens = cotangents[0][0].shape[1]
    strip = strip_of(width)
    cuts = [[piece.shape[0] for piece in pieces] for pieces in cotangents]
    rows = sum(sum(cut) for cut in cuts)
    block = max(row_block(count, 128) for cut in cuts for count in cut)
    args, aliases, outs = list(x_pieces), {}, []
    for pieces, state in zip(cotangents, states):
        args += pieces
        aliases[len(args)] = len(outs) + 1
        aliases[len(args) + 1] = len(outs) + 2
        args += state
        shape = state[0].shape
        outs += [pltpu.VMEM(shape, jnp.bfloat16)] * 2
        outs += [jax.ShapeDtypeStruct(shape, jnp.bfloat16)] * 2
    vmem = pl.BlockSpec(memory_space=pltpu.VMEM)
    hbm = pl.BlockSpec(memory_space=pl.ANY)
    done = pl.pallas_call(
        functools.partial(adam_kernel, strip, len(x_pieces), cuts),
        in_specs=[vmem] * len(args),
        out_specs=[vmem] + [vmem, vmem, hbm, hbm] * len(states),
        out_shape=[jax.ShapeDtypeStruct((1, rows), jnp.float32), *outs],
        input_output_aliases=aliases,
        scratch_shapes=[
            pltpu.VMEM((block, strip), jnp.float32),
            pltpu.VMEM((block, strip), jnp.float32),
            pltpu.VMEM((2, block, width), jnp.bfloat16),
            pltpu.VMEM((2, block, width), jnp.bfloat16),
            pltpu.VMEM((block, 128), jnp.float32),
            pltpu.SemaphoreType.DMA((2, 2)),
        ],
        compiler_params=with_vmem(12),
        cost_estimate=pl.CostEstimate(
            flops=2 * tokens * rows * width, bytes_accessed=4 * rows * width, transcendentals=0
        ),
        name="adam",
    )(*(pltpu.with_memory_space_constraint(array, pltpu.VMEM) for array in args))
    return done[0], [done[at : at + 4] for at in range(1, len(done), 4)]


def finish_kernel(count, whole_width, matrices, *refs):
    powers, refs = refs[:count], refs[count:]
    parts, outputs, (buffer, sems) = refs[: 2 * matrices], refs[-2 - matrices : -2], refs[-2:]
    slots = buffer.shape[0]
    base = 0
    for which, out_ref in enumerate(outputs):
        hi_ref, lo_ref = parts[2 * which : 2 * which + 2]
        rows, width = hi_ref.shape
        block = row_block(rows, 128)
        total = rows // block

        def one_block(at, base=base, block=block, total=total):
            slot = at % slots
            place = pl.ds(at * block, block)
            if total > slots:

                @pl.when(at >= slots)
                def _():
                    for copy in write_back([buffer], [out_ref], sems, slot, place):
                        copy.wait()

            lanes = pl.ds(base + at * block, block)
            power = powers[0][:, lanes]
            for other in powers[1:]:
                power = power + other[:, lanes]
            scale = 1.0 / jnp.sqrt(power / whole_width + eps_norm)
            scale = jnp.broadcast_to(scale, (128, block)).T
            for row in range(0, block, 16):
                inside = slice(row, row + 16)
                tile = pl.ds(at * block + row, 16)
                for lane in range(0, width, 128):
                    columns = slice(lane, lane + 128)
                    step = hi_ref[tile, columns].astype(jnp.float32)
                    step = step + lo_ref[tile, columns].astype(jnp.float32)
                    buffer[slot, inside, columns] = (step * scale[inside]).astype(jnp.bfloat16)
            for copy in write_back([buffer], [out_ref], sems, slot, place):
                copy.start()

        over_blocks(total, one_block)
        for at in range(max(0, total - slots), total):
            place = pl.ds(at * block, block)
            for copy in write_back([buffer], [out_ref], sems, at % slots, place):
                copy.wait()
        base += rows


def finish_rows(parts, powers, whole_width, after):
    shapes = [array.shape for array in parts[::2]]
    width = shapes[0][1]
    block = max(row_block(shape[0], 128) for shape in shapes)
    vmem = pl.BlockSpec(memory_space=pltpu.VMEM)
    return pl.pallas_call(
        functools.partial(finish_kernel, len(powers), whole_width, len(shapes)),
        in_specs=[vmem] * (len(powers) + len(parts))
        + [pl.BlockSpec(memory_space=pl.ANY)] * len(after),
        out_specs=[pl.BlockSpec(memory_space=pl.ANY)] * len(shapes),
        out_shape=[jax.ShapeDtypeStruct(shape, jnp.bfloat16) for shape in shapes],
        scratch_shapes=[
            pltpu.VMEM((4, block, width), jnp.bfloat16),
            pltpu.SemaphoreType.DMA((4, 1)),
        ],
        compiler_params=with_vmem(8),
        cost_estimate=pl.CostEstimate(
            flops=sum(2 * rows * width for rows, _ in shapes),
            bytes_accessed=sum(2 * rows * width for rows, _ in shapes),
            transcendentals=0,
        ),
        name="finish",
    )(
        *powers,
        *(pltpu.with_memory_space_constraint(array, pltpu.VMEM) for array in parts),
        *(pltpu.with_memory_space_constraint(array, pltpu.HBM) for array in after),
    )


def swap(array, axis, bit):
    return lax.ppermute(array, axis, [(at, at ^ bit) for at in range(lax.axis_size(axis))])


def from_others(pair, axis):
    bit = lax.axis_size(axis) // 2
    got = {0: pair[0], bit: pair[1]}
    while bit > 1:
        bit //= 2
        for turn in list(got):
            got[turn ^ bit] = swap(got[turn], axis, bit)
    return [got[turn] for turn in range(len(got))]


def straight_from_others(array, axis):
    size = lax.axis_size(axis)
    return [array] + [
        lax.ppermute(array, axis, [(at, at ^ turn) for at in range(size)])
        for turn in range(1, size)
    ]


def per_device(
    layer_input,
    query_cotangent,
    key_cotangent,
    up_cotangent,
    query_weight,
    key_weight,
    up_weight,
    moment_query,
    moment_key,
    moment_up,
    second_query,
    second_key,
    second_up,
):
    groups = lax.axis_size("dp")
    cols = lax.axis_size("col")
    part = layer_input.shape[0] // cols
    whole_width = layer_input.shape[1] * cols
    states = (
        (query_weight, moment_query, second_query),
        (key_weight, moment_key, second_key),
        (up_weight, moment_up, second_up),
    )
    place = jnp.stack([lax.axis_index("col"), lax.axis_index("dp")]).astype(jnp.int32)
    plan = [[(2, 0, up_weight.shape[0])]]
    plan.append([(which, 0, states[which][0].shape[0]) for which in (0, 1)])
    packed = pack((query_cotangent, key_cotangent, up_cotangent), plan, groups, part, place)
    one, two = ring_step(layer_input, layer_input, "dp")
    chunk, one, two = join((packed[0], one, two))
    behind, ahead = [layer_input, one], [layer_input, two]
    owned = lax.all_to_all(chunk, "dp", split_axis=0, concat_axis=0, tiled=True)
    one, two = ring_step(one, two, "dp")
    owned, one, two, chunk = join((owned, one, two, packed[1]))
    behind.append(one)
    ahead.append(two)
    swaps = [(owned, swap(owned, "col", cols // 2))]
    owned = lax.all_to_all(chunk, "dp", split_axis=0, concat_axis=0, tiled=True)
    one, two = ring_step(one, two, "dp")
    owned, one, two = join((owned, one, two), (swaps[0][1],))
    behind.append(one)
    ahead.append(two)
    swaps.append((owned, swap(owned, "col", cols // 2)))
    while 2 * len(behind) < groups:
        one, two = ring_step(one, two, "dp")
        behind.append(one)
        ahead.append(two)
    one, two = halves(one, two)
    middle = ring_step(one, two, "dp")
    *held, loaded = preload([array for state in states for array in state], one)
    held = [held[at : at + 3] for at in range(0, len(held), 3)]
    swaps[1] = join(swaps[1], (loaded, *middle))
    x_pieces = [layer_input, *ahead[1:], *middle, *behind[:0:-1]]
    cotangents = [[], [], []]
    for got, pieces in zip(swaps, plan):
        every = unpack(
            from_others(got, "col"), [high - low for _, low, high in pieces], place
        )
        for (which, _, _), cotangent in zip(pieces, every):
            cotangents[which].append(cotangent)
    updated = [None] * 3
    moments = [None] * 3
    passes = []
    for group in ((2,), (0, 1)):
        power, made = adam_pass(
            x_pieces, [cotangents[which] for which in group], [held[which] for which in group]
        )
        passes.append((group, straight_from_others(power, "col"), made))
    for group, powers, made in passes:
        parts = [array for done in made for array in done[:2]]
        after = [array for array in updated if array is not None]
        finished = finish_rows(parts, powers, whole_width, after)
        for which, done, array in zip(group, made, finished):
            updated[which] = array
            moments[which] = done[2:]
    return (*updated, *(done[0] for done in moments), *(done[1] for done in moments))


def solution(mesh):
    tokens_split = P("dp", None)
    split = P("dp", "col")
    return jax.shard_map(
        per_device,
        mesh=mesh,
        in_specs=(split, *(tokens_split,) * 3, *(split,) * 9),
        out_specs=(split,) * 9,
        check_vma=False,
    )
```

```python
import functools

import jax
import jax.numpy as jnp
from jax import lax
from jax.experimental import pallas as pl
from jax.experimental.pallas import tpu as pltpu
from jax.sharding import PartitionSpec as P

beta_one = 0.9
beta_two = 0.95
rate = 0.1
eps_adam = 1e-08
eps_norm = 1e-06


def with_vmem(mebibytes):
    return pltpu.CompilerParams(vmem_limit_bytes=mebibytes * 1024 * 1024)


def row_block(rows, largest=256):
    for block in range(largest, 0, -128):
        if rows % block == 0:
            return block
    return rows


def ring_order(groups):
    return [*range(0, groups, 2), *range(groups - 1 - groups % 2, 0, -2)]


def ring_place(at, groups):
    return jnp.where(at % 2 == 0, at // 2, groups - 1 - at // 2)


def pack_kernel(plan, groups, at_ref, *refs):
    inputs, outputs = refs[: -len(plan)], refs[-len(plan) :]
    for pieces, out_ref in zip(plan, outputs):
        start = 0
        for which, low, high in pieces:
            ref = inputs[which]
            rows = ref.shape[1] // groups
            for group in range(groups):
                out_ref[group, :, start : start + high - low] = ref[
                    :, group * rows + low : group * rows + high
                ]
            start += high - low


def pack(cotangents, plan, groups, part, place):
    outs = [
        jax.ShapeDtypeStruct(
            (groups, part, sum(high - low for _, low, high in pieces)), jnp.bfloat16
        )
        for pieces in plan
    ]
    return pl.pallas_call(
        functools.partial(pack_kernel, plan, groups),
        grid_spec=pltpu.PrefetchScalarGridSpec(
            num_scalar_prefetch=1,
            grid=(1,),
            in_specs=[
                pl.BlockSpec((part, array.shape[1]), lambda i, at: (at[0], 0))
                for array in cotangents
            ],
            out_specs=[pl.BlockSpec(out.shape, lambda i, at: (0, 0, 0)) for out in outs],
        ),
        out_shape=outs,
        compiler_params=with_vmem(16),
        cost_estimate=pl.CostEstimate(
            flops=0,
            bytes_accessed=4 * part * sum(array.shape[1] for array in cotangents),
            transcendentals=0,
        ),
        name="pack",
    )(place, *(pltpu.with_memory_space_constraint(array, pltpu.HBM) for array in cotangents))


def halves_kernel(one_ref, two_ref, first_ref, last_ref):
    half = first_ref.shape[0]
    first_ref[...] = one_ref[:half]
    last_ref[...] = two_ref[half:]


def halves(one, two):
    half = jax.ShapeDtypeStruct((one.shape[0] // 2, one.shape[1]), one.dtype)
    vmem = pl.BlockSpec(memory_space=pltpu.VMEM)
    return pl.pallas_call(
        halves_kernel,
        in_specs=[vmem] * 2,
        out_specs=[vmem] * 2,
        out_shape=[half] * 2,
        compiler_params=with_vmem(4),
        cost_estimate=pl.CostEstimate(
            flops=0, bytes_accessed=4 * one.size, transcendentals=0
        ),
        name="halves",
    )(one, two)


def ring_paths(groups):
    order = ring_order(groups)
    onward = list(zip(order, order[1:] + order[:1]))
    return onward, [(to, at) for at, to in onward]


def ring_step(one, two, axis):
    onward, back = ring_paths(lax.axis_size(axis))
    return lax.ppermute(one, axis, onward), lax.ppermute(two, axis, back)


def unpack_kernel(count, at_ref, *refs):
    pieces, outputs, orders = refs[:count], refs[count:-2], refs[-2:]
    groups = pieces[0].shape[0]
    here = ring_place(at_ref[1], groups)
    slots = [(ring_place(group, groups) - here + groups) % groups for group in range(groups)]
    low = 0
    for out_ref in outputs:
        rows = out_ref.shape[0]
        for start in range(0, rows, 128):
            high = min(start + 128, rows)
            order = orders[start // 128 % 2]
            for group, slot in enumerate(slots):
                for turn, piece in enumerate(pieces):
                    order[slot * count + (at_ref[0] ^ turn), :, : high - start] = piece[
                        group, :, low + start : low + high
                    ]
            out_ref[start:high] = order[...].reshape(-1, 128).T[: high - start]
        low += rows


def unpack(pieces, row_counts, place):
    groups, part, rows = pieces[0].shape
    tokens = groups * part * len(pieces)
    vmem = pl.BlockSpec(memory_space=pltpu.VMEM)
    order = pltpu.VMEM((groups * len(pieces), part, 128), jnp.bfloat16)
    return pl.pallas_call(
        functools.partial(unpack_kernel, len(pieces)),
        in_specs=[pl.BlockSpec(memory_space=pltpu.SMEM)] + [vmem] * len(pieces),
        out_specs=[vmem] * len(row_counts),
        out_shape=[pltpu.VMEM((count, tokens), jnp.bfloat16) for count in row_counts],
        scratch_shapes=[order, order],
        compiler_params=with_vmem(4 + 6 * tokens * 256 // 2**20),
        cost_estimate=pl.CostEstimate(
            flops=0, bytes_accessed=4 * tokens * rows, transcendentals=0
        ),
        name="unpack",
    )(place, *pieces)


def join_kernel(*refs):
    pass


def join(arrays, after=()):
    count = len(arrays)
    hbm = pl.BlockSpec(memory_space=pl.ANY)
    return pl.pallas_call(
        join_kernel,
        in_specs=[hbm] * (count + len(after)),
        out_specs=[hbm] * count,
        out_shape=[jax.ShapeDtypeStruct(array.shape, array.dtype) for array in arrays],
        input_output_aliases={at: at for at in range(count)},
        compiler_params=with_vmem(1),
        name="join",
    )(*arrays, *after)


def preload_kernel(*refs):
    count = (len(refs) - 3) // 2
    token, sems = refs[-2:]
    outputs = refs[count + 1 :]
    copies = [pltpu.make_async_copy(refs[at], outputs[at], sems.at[at]) for at in range(count)]
    token[...] = jnp.zeros_like(token)
    for copy in copies:
        copy.start()
    for copy in copies:
        copy.wait()


def preload(arrays, after):
    return pl.pallas_call(
        preload_kernel,
        in_specs=[pl.BlockSpec(memory_space=pl.ANY)] * (len(arrays) + 1),
        out_specs=[pl.BlockSpec(memory_space=pltpu.VMEM)] * (len(arrays) + 1),
        out_shape=[pltpu.VMEM(array.shape, array.dtype) for array in arrays]
        + [jax.ShapeDtypeStruct((8, 128), jnp.float32)],
        scratch_shapes=[pltpu.SemaphoreType.DMA((len(arrays),))],
        compiler_params=with_vmem(4),
        cost_estimate=pl.CostEstimate(
            flops=0, bytes_accessed=sum(2 * array.size for array in arrays), transcendentals=0
        ),
        name="preload",
    )(*(pltpu.with_memory_space_constraint(array, pltpu.HBM) for array in arrays), after)


def write_back(buffers, outputs, sems, slot, at):
    return [
        pltpu.make_async_copy(buffer.at[slot, : at.size], out.at[at], sems.at[slot, which])
        for which, (buffer, out) in enumerate(zip(buffers, outputs))
    ]


def over_blocks(count, body):
    if count == 1:
        body(0)
    else:
        pl.loop(0, count)(body)


def update_tile(grad, weight, moment, second):
    first = beta_one * moment.astype(jnp.float32) + (1.0 - beta_one) * grad
    square = beta_two * second.astype(jnp.float32) + (1.0 - beta_two) * grad * grad
    inverse = lax.rsqrt(square)
    root = square * inverse + eps_adam
    inverse = inverse * (2.0 - root * inverse)
    return first, square, weight.astype(jnp.float32) - rate * first * inverse


def adam_kernel(strip, count_x, cuts, *refs):
    refs = list(refs)
    take = lambda count: [refs.pop(0) for _ in range(count)]
    x_refs = take(count_x)
    ins = [(take(len(cut)), *take(3)) for cut in cuts]
    power_ref = refs.pop(0)
    outs = [take(4) for _ in cuts]
    grads, buffers, power_sum, sems = (refs[0], refs[1]), (refs[2], refs[3]), refs[4], refs[5]
    width = x_refs[0].shape[1]
    strips = width // strip
    base = 0
    for cut, (c_refs, w_ref, m_ref, v_ref), (hi_ref, lo_ref, *moments) in zip(cuts, ins, outs):
        low = 0
        for c_ref, rows in zip(c_refs, cut):
            block = row_block(rows, 128)
            count = rows // block

            def multiply(at, which, c_ref=c_ref, block=block):
                lhs = c_ref[pl.ds(at * block, block), :]
                columns = slice(which * strip, (which + 1) * strip)
                rhs = jnp.concatenate([x_ref[:, columns] for x_ref in x_refs], axis=0)
                grads[which % 2][:block] = jnp.dot(lhs, rhs, preferred_element_type=jnp.float32)

            def one_block(at, low=low, base=base, count=count, block=block, multiply=multiply):
                slot = at % 2
                place = pl.ds(low + at * block, block)
                if count > 2:

                    @pl.when(at >= 2)
                    def _():
                        for copy in write_back(buffers, moments, sems, slot, place):
                            copy.wait()

                for which in range(strips):
                    if which + 1 < strips:
                        multiply(at, which + 1)
                    elif count > 1:
                        multiply(jnp.minimum(at + 1, count - 1), 0)
                    columns = slice(which * strip, (which + 1) * strip)
                    for row in range(0, block, 16):
                        inside = slice(row, row + 16)
                        tile = pl.ds(low + at * block + row, 16)
                        first, square, step = update_tile(
                            grads[which % 2][inside],
                            w_ref[tile, columns],
                            m_ref[tile, columns],
                            v_ref[tile, columns],
                        )
                        buffers[0][slot, inside, columns] = first.astype(jnp.bfloat16)
                        buffers[1][slot, inside, columns] = square.astype(jnp.bfloat16)
                        hi = step.astype(jnp.bfloat16)
                        hi_ref[tile, columns] = hi
                        lo_ref[tile, columns] = (step - hi.astype(jnp.float32)).astype(
                            jnp.bfloat16
                        )
                        power = step[:, :128] * step[:, :128]
                        for lane in range(128, strip, 128):
                            power += step[:, lane : lane + 128] * step[:, lane : lane + 128]
                        if which:
                            power += power_sum[inside]
                        power_sum[inside] = power
                power_ref[:, pl.ds(base + low + at * block, block)] = jnp.sum(
                    power_sum[:block].T, axis=0, keepdims=True
                )
                for copy in write_back(buffers, moments, sems, slot, place):
                    copy.start()

            multiply(0, 0)
            over_blocks(count, one_block)
            for at in range(max(0, count - 2), count):
                place = pl.ds(low + at * block, block)
                for copy in write_back(buffers, moments, sems, at % 2, place):
                    copy.wait()
            low += rows
        base += low


def strip_of(width, largest=256):
    for strip in range(largest, 0, -128):
        if width % (2 * strip) == 0:
            return strip


def adam_pass(x_pieces, cotangents, states):
    width = x_pieces[0].shape[1]
    tokens = cotangents[0][0].shape[1]
    strip = strip_of(width)
    cuts = [[piece.shape[0] for piece in pieces] for pieces in cotangents]
    rows = sum(sum(cut) for cut in cuts)
    block = max(row_block(count, 128) for cut in cuts for count in cut)
    args, aliases, outs = list(x_pieces), {}, []
    for pieces, state in zip(cotangents, states):
        args += pieces
        aliases[len(args)] = len(outs) + 1
        aliases[len(args) + 1] = len(outs) + 2
        args += state
        shape = state[0].shape
        outs += [pltpu.VMEM(shape, jnp.bfloat16)] * 2
        outs += [jax.ShapeDtypeStruct(shape, jnp.bfloat16)] * 2
    vmem = pl.BlockSpec(memory_space=pltpu.VMEM)
    hbm = pl.BlockSpec(memory_space=pl.ANY)
    done = pl.pallas_call(
        functools.partial(adam_kernel, strip, len(x_pieces), cuts),
        in_specs=[vmem] * len(args),
        out_specs=[vmem] + [vmem, vmem, hbm, hbm] * len(states),
        out_shape=[jax.ShapeDtypeStruct((1, rows), jnp.float32), *outs],
        input_output_aliases=aliases,
        scratch_shapes=[
            pltpu.VMEM((block, strip), jnp.float32),
            pltpu.VMEM((block, strip), jnp.float32),
            pltpu.VMEM((2, block, width), jnp.bfloat16),
            pltpu.VMEM((2, block, width), jnp.bfloat16),
            pltpu.VMEM((block, 128), jnp.float32),
            pltpu.SemaphoreType.DMA((2, 2)),
        ],
        compiler_params=with_vmem(12),
        cost_estimate=pl.CostEstimate(
            flops=2 * tokens * rows * width, bytes_accessed=4 * rows * width, transcendentals=0
        ),
        name="adam",
    )(*(pltpu.with_memory_space_constraint(array, pltpu.VMEM) for array in args))
    return done[0], [done[at : at + 4] for at in range(1, len(done), 4)]


def finish_kernel(count, whole_width, matrices, *refs):
    powers, refs = refs[:count], refs[count:]
    parts, outputs, (buffer, sems) = refs[: 2 * matrices], refs[-2 - matrices : -2], refs[-2:]
    slots = buffer.shape[0]
    base = 0
    for which, out_ref in enumerate(outputs):
        hi_ref, lo_ref = parts[2 * which : 2 * which + 2]
        rows, width = hi_ref.shape
        block = row_block(rows, 128)
        total = rows // block

        def one_block(at, base=base, block=block, total=total):
            slot = at % slots
            place = pl.ds(at * block, block)
            if total > slots:

                @pl.when(at >= slots)
                def _():
                    for copy in write_back([buffer], [out_ref], sems, slot, place):
                        copy.wait()

            lanes = pl.ds(base + at * block, block)
            power = powers[0][:, lanes]
            for other in powers[1:]:
                power = power + other[:, lanes]
            scale = 1.0 / jnp.sqrt(power / whole_width + eps_norm)
            scale = jnp.broadcast_to(scale, (128, block)).T
            for row in range(0, block, 16):
                inside = slice(row, row + 16)
                tile = pl.ds(at * block + row, 16)
                for lane in range(0, width, 128):
                    columns = slice(lane, lane + 128)
                    step = hi_ref[tile, columns].astype(jnp.float32)
                    step = step + lo_ref[tile, columns].astype(jnp.float32)
                    buffer[slot, inside, columns] = (step * scale[inside]).astype(jnp.bfloat16)
            for copy in write_back([buffer], [out_ref], sems, slot, place):
                copy.start()

        over_blocks(total, one_block)
        for at in range(max(0, total - slots), total):
            place = pl.ds(at * block, block)
            for copy in write_back([buffer], [out_ref], sems, at % slots, place):
                copy.wait()
        base += rows


def finish_rows(parts, powers, whole_width, after):
    shapes = [array.shape for array in parts[::2]]
    width = shapes[0][1]
    block = max(row_block(shape[0], 128) for shape in shapes)
    vmem = pl.BlockSpec(memory_space=pltpu.VMEM)
    return pl.pallas_call(
        functools.partial(finish_kernel, len(powers), whole_width, len(shapes)),
        in_specs=[vmem] * (len(powers) + len(parts))
        + [pl.BlockSpec(memory_space=pl.ANY)] * len(after),
        out_specs=[pl.BlockSpec(memory_space=pl.ANY)] * len(shapes),
        out_shape=[jax.ShapeDtypeStruct(shape, jnp.bfloat16) for shape in shapes],
        scratch_shapes=[
            pltpu.VMEM((4, block, width), jnp.bfloat16),
            pltpu.SemaphoreType.DMA((4, 1)),
        ],
        compiler_params=with_vmem(8),
        cost_estimate=pl.CostEstimate(
            flops=sum(2 * rows * width for rows, _ in shapes),
            bytes_accessed=sum(2 * rows * width for rows, _ in shapes),
            transcendentals=0,
        ),
        name="finish",
    )(
        *powers,
        *(pltpu.with_memory_space_constraint(array, pltpu.VMEM) for array in parts),
        *(pltpu.with_memory_space_constraint(array, pltpu.HBM) for array in after),
    )


def swap(array, axis, bit):
    return lax.ppermute(array, axis, [(at, at ^ bit) for at in range(lax.axis_size(axis))])


def from_others(pair, axis):
    bit = lax.axis_size(axis) // 2
    got = {0: pair[0], bit: pair[1]}
    while bit > 1:
        bit //= 2
        for turn in list(got):
            got[turn ^ bit] = swap(got[turn], axis, bit)
    return [got[turn] for turn in range(len(got))]


def straight_from_others(array, axis):
    size = lax.axis_size(axis)
    return [array] + [
        lax.ppermute(array, axis, [(at, at ^ turn) for at in range(size)])
        for turn in range(1, size)
    ]


def per_device(
    layer_input,
    query_cotangent,
    key_cotangent,
    up_cotangent,
    query_weight,
    key_weight,
    up_weight,
    moment_query,
    moment_key,
    moment_up,
    second_query,
    second_key,
    second_up,
):
    groups = lax.axis_size("dp")
    cols = lax.axis_size("col")
    part = layer_input.shape[0] // cols
    whole_width = layer_input.shape[1] * cols
    states = (
        (query_weight, moment_query, second_query),
        (key_weight, moment_key, second_key),
        (up_weight, moment_up, second_up),
    )
    place = jnp.stack([lax.axis_index("col"), lax.axis_index("dp")]).astype(jnp.int32)
    plan = [[(which, 0, states[which][0].shape[0]) for which in (0, 1)]]
    plan.append([(2, 0, up_weight.shape[0])])
    packed = pack((query_cotangent, key_cotangent, up_cotangent), plan, groups, part, place)
    one, two = ring_step(layer_input, layer_input, "dp")
    owned = lax.all_to_all(packed[0], "dp", split_axis=0, concat_axis=0, tiled=True)
    owned, one, two, chunk = join((owned, one, two, packed[1]))
    behind, ahead = [layer_input, one], [layer_input, two]
    swaps = [(owned, swap(owned, "col", cols // 2))]
    owned = lax.all_to_all(chunk, "dp", split_axis=0, concat_axis=0, tiled=True)
    one, two = ring_step(one, two, "dp")
    owned, one, two = join((owned, one, two), (swaps[0][1],))
    behind.append(one)
    ahead.append(two)
    swaps.append((owned, swap(owned, "col", cols // 2)))
    *held, loaded = preload([array for state in states for array in state], owned)
    held = [held[at : at + 3] for at in range(0, len(held), 3)]
    one, two = join(ring_step(one, two, "dp"), (loaded,))
    behind.append(one)
    ahead.append(two)
    while 2 * len(behind) < groups:
        one, two = ring_step(one, two, "dp")
        behind.append(one)
        ahead.append(two)
    middle = ring_step(*halves(one, two), "dp")
    swaps[1] = join(swaps[1], middle)
    x_pieces = [layer_input, *ahead[1:], *middle, *behind[:0:-1]]
    cotangents = [[], [], []]
    for got, pieces in zip(swaps, plan):
        every = unpack(
            from_others(got, "col"), [high - low for _, low, high in pieces], place
        )
        for (which, _, _), cotangent in zip(pieces, every):
            cotangents[which].append(cotangent)
    updated = [None] * 3
    moments = [None] * 3
    passes = []
    for group in ((2,), (0, 1)):
        power, made = adam_pass(
            x_pieces, [cotangents[which] for which in group], [held[which] for which in group]
        )
        passes.append((group, straight_from_others(power, "col"), made))
    for group, powers, made in passes:
        parts = [array for done in made for array in done[:2]]
        after = [array for array in updated if array is not None]
        finished = finish_rows(parts, powers, whole_width, after)
        for which, done, array in zip(group, made, finished):
            updated[which] = array
            moments[which] = done[2:]
    return (*updated, *(done[0] for done in moments), *(done[1] for done in moments))


def solution(mesh):
    tokens_split = P("dp", None)
    split = P("dp", "col")
    return jax.shard_map(
        per_device,
        mesh=mesh,
        in_specs=(split, *(tokens_split,) * 3, *(split,) * 9),
        out_specs=(split,) * 9,
        check_vma=False,
    )
```

```python
import functools

import jax
import jax.numpy as jnp
from jax import lax
from jax.experimental import pallas as pl
from jax.experimental.pallas import tpu as pltpu
from jax.sharding import PartitionSpec as P

beta_one = 0.9
beta_two = 0.95
rate = 0.1
eps_adam = 1e-08
eps_norm = 1e-06


def with_vmem(mebibytes):
    return pltpu.CompilerParams(vmem_limit_bytes=mebibytes * 1024 * 1024)


def row_block(rows, largest=256):
    for block in range(largest, 0, -128):
        if rows % block == 0:
            return block
    return rows


def ring_order(groups):
    return [*range(0, groups, 2), *range(groups - 1 - groups % 2, 0, -2)]


def ring_place(at, groups):
    return jnp.where(at % 2 == 0, at // 2, groups - 1 - at // 2)


def pack_kernel(plan, groups, at_ref, *refs):
    inputs, outputs = refs[: -len(plan)], refs[-len(plan) :]
    for pieces, out_ref in zip(plan, outputs):
        start = 0
        for which, low, high in pieces:
            ref = inputs[which]
            rows = ref.shape[1] // groups
            for group in range(groups):
                out_ref[group, :, start : start + high - low] = ref[
                    :, group * rows + low : group * rows + high
                ]
            start += high - low


def pack(cotangents, plan, groups, part, place):
    outs = [
        jax.ShapeDtypeStruct(
            (groups, part, sum(high - low for _, low, high in pieces)), jnp.bfloat16
        )
        for pieces in plan
    ]
    return pl.pallas_call(
        functools.partial(pack_kernel, plan, groups),
        grid_spec=pltpu.PrefetchScalarGridSpec(
            num_scalar_prefetch=1,
            grid=(1,),
            in_specs=[
                pl.BlockSpec((part, array.shape[1]), lambda i, at: (at[0], 0))
                for array in cotangents
            ],
            out_specs=[pl.BlockSpec(out.shape, lambda i, at: (0, 0, 0)) for out in outs],
        ),
        out_shape=outs,
        compiler_params=with_vmem(16),
        cost_estimate=pl.CostEstimate(
            flops=0,
            bytes_accessed=4 * part * sum(array.shape[1] for array in cotangents),
            transcendentals=0,
        ),
        name="pack",
    )(place, *(pltpu.with_memory_space_constraint(array, pltpu.HBM) for array in cotangents))


def halves_kernel(one_ref, two_ref, first_ref, last_ref):
    half = first_ref.shape[0]
    first_ref[...] = one_ref[:half]
    last_ref[...] = two_ref[half:]


def halves(one, two):
    half = jax.ShapeDtypeStruct((one.shape[0] // 2, one.shape[1]), one.dtype)
    vmem = pl.BlockSpec(memory_space=pltpu.VMEM)
    return pl.pallas_call(
        halves_kernel,
        in_specs=[vmem] * 2,
        out_specs=[vmem] * 2,
        out_shape=[half] * 2,
        compiler_params=with_vmem(4),
        cost_estimate=pl.CostEstimate(
            flops=0, bytes_accessed=4 * one.size, transcendentals=0
        ),
        name="halves",
    )(one, two)


def ring_paths(groups):
    order = ring_order(groups)
    onward = list(zip(order, order[1:] + order[:1]))
    return onward, [(to, at) for at, to in onward]


def ring_step(one, two, axis):
    onward, back = ring_paths(lax.axis_size(axis))
    return lax.ppermute(one, axis, onward), lax.ppermute(two, axis, back)


def unpack_kernel(count, at_ref, *refs):
    pieces, outputs, orders = refs[:count], refs[count:-2], refs[-2:]
    groups = pieces[0].shape[0]
    here = ring_place(at_ref[1], groups)
    slots = [(ring_place(group, groups) - here + groups) % groups for group in range(groups)]
    low = 0
    for out_ref in outputs:
        rows = out_ref.shape[0]
        for start in range(0, rows, 128):
            high = min(start + 128, rows)
            order = orders[start // 128 % 2]
            for group, slot in enumerate(slots):
                for turn, piece in enumerate(pieces):
                    order[slot * count + (at_ref[0] ^ turn), :, : high - start] = piece[
                        group, :, low + start : low + high
                    ]
            out_ref[start:high] = order[...].reshape(-1, 128).T[: high - start]
        low += rows


def unpack(pieces, row_counts, place):
    groups, part, rows = pieces[0].shape
    tokens = groups * part * len(pieces)
    vmem = pl.BlockSpec(memory_space=pltpu.VMEM)
    order = pltpu.VMEM((groups * len(pieces), part, 128), jnp.bfloat16)
    return pl.pallas_call(
        functools.partial(unpack_kernel, len(pieces)),
        in_specs=[pl.BlockSpec(memory_space=pltpu.SMEM)] + [vmem] * len(pieces),
        out_specs=[vmem] * len(row_counts),
        out_shape=[pltpu.VMEM((count, tokens), jnp.bfloat16) for count in row_counts],
        scratch_shapes=[order, order],
        compiler_params=with_vmem(4 + 6 * tokens * 256 // 2**20),
        cost_estimate=pl.CostEstimate(
            flops=0, bytes_accessed=4 * tokens * rows, transcendentals=0
        ),
        name="unpack",
    )(place, *pieces)


def join_kernel(*refs):
    pass


def join(arrays, after=()):
    count = len(arrays)
    hbm = pl.BlockSpec(memory_space=pl.ANY)
    return pl.pallas_call(
        join_kernel,
        in_specs=[hbm] * (count + len(after)),
        out_specs=[hbm] * count,
        out_shape=[jax.ShapeDtypeStruct(array.shape, array.dtype) for array in arrays],
        input_output_aliases={at: at for at in range(count)},
        compiler_params=with_vmem(1),
        name="join",
    )(*arrays, *after)


def preload_kernel(*refs):
    count = (len(refs) - 3) // 2
    token, sems = refs[-2:]
    outputs = refs[count + 1 :]
    copies = [pltpu.make_async_copy(refs[at], outputs[at], sems.at[at]) for at in range(count)]
    token[...] = jnp.zeros_like(token)
    for copy in copies:
        copy.start()
    for copy in copies:
        copy.wait()


def preload(arrays, after):
    return pl.pallas_call(
        preload_kernel,
        in_specs=[pl.BlockSpec(memory_space=pl.ANY)] * (len(arrays) + 1),
        out_specs=[pl.BlockSpec(memory_space=pltpu.VMEM)] * (len(arrays) + 1),
        out_shape=[pltpu.VMEM(array.shape, array.dtype) for array in arrays]
        + [jax.ShapeDtypeStruct((8, 128), jnp.float32)],
        scratch_shapes=[pltpu.SemaphoreType.DMA((len(arrays),))],
        compiler_params=with_vmem(4),
        cost_estimate=pl.CostEstimate(
            flops=0, bytes_accessed=sum(2 * array.size for array in arrays), transcendentals=0
        ),
        name="preload",
    )(*(pltpu.with_memory_space_constraint(array, pltpu.HBM) for array in arrays), after)


def write_back(buffers, outputs, sems, slot, at):
    return [
        pltpu.make_async_copy(buffer.at[slot, : at.size], out.at[at], sems.at[slot, which])
        for which, (buffer, out) in enumerate(zip(buffers, outputs))
    ]


def over_blocks(count, body):
    if count == 1:
        body(0)
    else:
        pl.loop(0, count)(body)


def update_tile(grad, weight, moment, second):
    first = beta_one * moment.astype(jnp.float32) + (1.0 - beta_one) * grad
    square = beta_two * second.astype(jnp.float32) + (1.0 - beta_two) * grad * grad
    inverse = lax.rsqrt(square)
    root = square * inverse + eps_adam
    inverse = inverse * (2.0 - root * inverse)
    return first, square, weight.astype(jnp.float32) - rate * first * inverse


def adam_kernel(strip, count_x, cuts, *refs):
    refs = list(refs)
    take = lambda count: [refs.pop(0) for _ in range(count)]
    x_refs = take(count_x)
    ins = [(take(len(cut)), *take(3)) for cut in cuts]
    power_ref = refs.pop(0)
    outs = [take(4) for _ in cuts]
    grads, buffers, power_sum, sems = (refs[0], refs[1]), (refs[2], refs[3]), refs[4], refs[5]
    width = x_refs[0].shape[1]
    strips = width // strip
    base = 0
    for cut, (c_refs, w_ref, m_ref, v_ref), (hi_ref, lo_ref, *moments) in zip(cuts, ins, outs):
        low = 0
        for c_ref, rows in zip(c_refs, cut):
            block = row_block(rows, 128)
            count = rows // block

            def multiply(at, which, c_ref=c_ref, block=block):
                lhs = c_ref[pl.ds(at * block, block), :]
                columns = slice(which * strip, (which + 1) * strip)
                rhs = jnp.concatenate([x_ref[:, columns] for x_ref in x_refs], axis=0)
                grads[which % 2][:block] = jnp.dot(lhs, rhs, preferred_element_type=jnp.float32)

            def one_block(at, low=low, base=base, count=count, block=block, multiply=multiply):
                slot = at % 2
                place = pl.ds(low + at * block, block)
                if count > 2:

                    @pl.when(at >= 2)
                    def _():
                        for copy in write_back(buffers, moments, sems, slot, place):
                            copy.wait()

                for which in range(strips):
                    if which + 1 < strips:
                        multiply(at, which + 1)
                    elif count > 1:
                        multiply(jnp.minimum(at + 1, count - 1), 0)
                    columns = slice(which * strip, (which + 1) * strip)
                    for row in range(0, block, 16):
                        inside = slice(row, row + 16)
                        tile = pl.ds(low + at * block + row, 16)
                        first, square, step = update_tile(
                            grads[which % 2][inside],
                            w_ref[tile, columns],
                            m_ref[tile, columns],
                            v_ref[tile, columns],
                        )
                        buffers[0][slot, inside, columns] = first.astype(jnp.bfloat16)
                        buffers[1][slot, inside, columns] = square.astype(jnp.bfloat16)
                        hi = step.astype(jnp.bfloat16)
                        hi_ref[tile, columns] = hi
                        lo_ref[tile, columns] = (step - hi.astype(jnp.float32)).astype(
                            jnp.bfloat16
                        )
                        power = step[:, :128] * step[:, :128]
                        for lane in range(128, strip, 128):
                            power += step[:, lane : lane + 128] * step[:, lane : lane + 128]
                        if which:
                            power += power_sum[inside]
                        power_sum[inside] = power
                power_ref[:, pl.ds(base + low + at * block, block)] = jnp.sum(
                    power_sum[:block].T, axis=0, keepdims=True
                )
                for copy in write_back(buffers, moments, sems, slot, place):
                    copy.start()

            multiply(0, 0)
            over_blocks(count, one_block)
            for at in range(max(0, count - 2), count):
                place = pl.ds(low + at * block, block)
                for copy in write_back(buffers, moments, sems, at % 2, place):
                    copy.wait()
            low += rows
        base += low


def strip_of(width, largest=256):
    for strip in range(largest, 0, -128):
        if width % (2 * strip) == 0:
            return strip


def adam_pass(x_pieces, cotangents, states):
    width = x_pieces[0].shape[1]
    tokens = cotangents[0][0].shape[1]
    strip = strip_of(width)
    cuts = [[piece.shape[0] for piece in pieces] for pieces in cotangents]
    rows = sum(sum(cut) for cut in cuts)
    block = max(row_block(count, 128) for cut in cuts for count in cut)
    args, aliases, outs = list(x_pieces), {}, []
    for pieces, state in zip(cotangents, states):
        args += pieces
        aliases[len(args)] = len(outs) + 1
        aliases[len(args) + 1] = len(outs) + 2
        args += state
        shape = state[0].shape
        outs += [pltpu.VMEM(shape, jnp.bfloat16)] * 2
        outs += [jax.ShapeDtypeStruct(shape, jnp.bfloat16)] * 2
    vmem = pl.BlockSpec(memory_space=pltpu.VMEM)
    hbm = pl.BlockSpec(memory_space=pl.ANY)
    done = pl.pallas_call(
        functools.partial(adam_kernel, strip, len(x_pieces), cuts),
        in_specs=[vmem] * len(args),
        out_specs=[vmem] + [vmem, vmem, hbm, hbm] * len(states),
        out_shape=[jax.ShapeDtypeStruct((1, rows), jnp.float32), *outs],
        input_output_aliases=aliases,
        scratch_shapes=[
            pltpu.VMEM((block, strip), jnp.float32),
            pltpu.VMEM((block, strip), jnp.float32),
            pltpu.VMEM((2, block, width), jnp.bfloat16),
            pltpu.VMEM((2, block, width), jnp.bfloat16),
            pltpu.VMEM((block, 128), jnp.float32),
            pltpu.SemaphoreType.DMA((2, 2)),
        ],
        compiler_params=with_vmem(12),
        cost_estimate=pl.CostEstimate(
            flops=2 * tokens * rows * width, bytes_accessed=4 * rows * width, transcendentals=0
        ),
        name="adam",
    )(*(pltpu.with_memory_space_constraint(array, pltpu.VMEM) for array in args))
    return done[0], [done[at : at + 4] for at in range(1, len(done), 4)]


def finish_kernel(count, whole_width, matrices, *refs):
    powers, refs = refs[:count], refs[count:]
    parts, outputs, (buffer, sems) = refs[: 2 * matrices], refs[-2 - matrices : -2], refs[-2:]
    slots = buffer.shape[0]
    base = 0
    for which, out_ref in enumerate(outputs):
        hi_ref, lo_ref = parts[2 * which : 2 * which + 2]
        rows, width = hi_ref.shape
        block = row_block(rows, 128)
        total = rows // block

        def one_block(at, base=base, block=block, total=total):
            slot = at % slots
            place = pl.ds(at * block, block)
            if total > slots:

                @pl.when(at >= slots)
                def _():
                    for copy in write_back([buffer], [out_ref], sems, slot, place):
                        copy.wait()

            lanes = pl.ds(base + at * block, block)
            power = powers[0][:, lanes]
            for other in powers[1:]:
                power = power + other[:, lanes]
            scale = 1.0 / jnp.sqrt(power / whole_width + eps_norm)
            scale = jnp.broadcast_to(scale, (128, block)).T
            for row in range(0, block, 16):
                inside = slice(row, row + 16)
                tile = pl.ds(at * block + row, 16)
                for lane in range(0, width, 128):
                    columns = slice(lane, lane + 128)
                    step = hi_ref[tile, columns].astype(jnp.float32)
                    step = step + lo_ref[tile, columns].astype(jnp.float32)
                    buffer[slot, inside, columns] = (step * scale[inside]).astype(jnp.bfloat16)
            for copy in write_back([buffer], [out_ref], sems, slot, place):
                copy.start()

        over_blocks(total, one_block)
        for at in range(max(0, total - slots), total):
            place = pl.ds(at * block, block)
            for copy in write_back([buffer], [out_ref], sems, at % slots, place):
                copy.wait()
        base += rows


def finish_rows(parts, powers, whole_width, after):
    shapes = [array.shape for array in parts[::2]]
    width = shapes[0][1]
    block = max(row_block(shape[0], 128) for shape in shapes)
    vmem = pl.BlockSpec(memory_space=pltpu.VMEM)
    return pl.pallas_call(
        functools.partial(finish_kernel, len(powers), whole_width, len(shapes)),
        in_specs=[vmem] * (len(powers) + len(parts))
        + [pl.BlockSpec(memory_space=pl.ANY)] * len(after),
        out_specs=[pl.BlockSpec(memory_space=pl.ANY)] * len(shapes),
        out_shape=[jax.ShapeDtypeStruct(shape, jnp.bfloat16) for shape in shapes],
        scratch_shapes=[
            pltpu.VMEM((4, block, width), jnp.bfloat16),
            pltpu.SemaphoreType.DMA((4, 1)),
        ],
        compiler_params=with_vmem(8),
        cost_estimate=pl.CostEstimate(
            flops=sum(2 * rows * width for rows, _ in shapes),
            bytes_accessed=sum(2 * rows * width for rows, _ in shapes),
            transcendentals=0,
        ),
        name="finish",
    )(
        *powers,
        *(pltpu.with_memory_space_constraint(array, pltpu.VMEM) for array in parts),
        *(pltpu.with_memory_space_constraint(array, pltpu.HBM) for array in after),
    )


def swap(array, axis, bit):
    return lax.ppermute(array, axis, [(at, at ^ bit) for at in range(lax.axis_size(axis))])


def from_others(pair, axis):
    bit = lax.axis_size(axis) // 2
    got = {0: pair[0], bit: pair[1]}
    while bit > 1:
        bit //= 2
        for turn in list(got):
            got[turn ^ bit] = swap(got[turn], axis, bit)
    return [got[turn] for turn in range(len(got))]


def straight_from_others(array, axis):
    size = lax.axis_size(axis)
    return [array] + [
        lax.ppermute(array, axis, [(at, at ^ turn) for at in range(size)])
        for turn in range(1, size)
    ]


def unpack_chunk(pair, pieces, place):
    return unpack(from_others(pair, "col"), [high - low for _, low, high in pieces], place)


def per_device(
    layer_input,
    query_cotangent,
    key_cotangent,
    up_cotangent,
    query_weight,
    key_weight,
    up_weight,
    moment_query,
    moment_key,
    moment_up,
    second_query,
    second_key,
    second_up,
):
    groups = lax.axis_size("dp")
    cols = lax.axis_size("col")
    part = layer_input.shape[0] // cols
    whole_width = layer_input.shape[1] * cols
    states = (
        (query_weight, moment_query, second_query),
        (key_weight, moment_key, second_key),
        (up_weight, moment_up, second_up),
    )
    place = jnp.stack([lax.axis_index("col"), lax.axis_index("dp")]).astype(jnp.int32)
    plan = [[(which, 0, states[which][0].shape[0]) for which in (0, 1)]]
    plan.append([(2, 0, up_weight.shape[0])])
    packed = pack((query_cotangent, key_cotangent, up_cotangent), plan, groups, part, place)
    one, two = ring_step(layer_input, layer_input, "dp")
    owned = lax.all_to_all(packed[0], "dp", split_axis=0, concat_axis=0, tiled=True)
    owned, one, two, chunk = join((owned, one, two, packed[1]))
    behind, ahead = [layer_input, one], [layer_input, two]
    swaps = [(owned, swap(owned, "col", cols // 2))]
    owned = lax.all_to_all(chunk, "dp", split_axis=0, concat_axis=0, tiled=True)
    one, two = ring_step(one, two, "dp")
    owned, one, two = join((owned, one, two), (swaps[0][1],))
    behind.append(one)
    ahead.append(two)
    swaps.append((owned, swap(owned, "col", cols // 2)))
    *held, loaded = preload([array for state in states for array in state], owned)
    held = [held[at : at + 3] for at in range(0, len(held), 3)]
    early = unpack_chunk(swaps[0], plan[0], place)
    one, two = join(ring_step(one, two, "dp"), (loaded, *early))
    behind.append(one)
    ahead.append(two)
    while 2 * len(behind) < groups:
        one, two = ring_step(one, two, "dp")
        behind.append(one)
        ahead.append(two)
    middle = ring_step(*halves(one, two), "dp")
    swaps[1] = join(swaps[1], middle)
    x_pieces = [layer_input, *ahead[1:], *middle, *behind[:0:-1]]
    cotangents = [[], [], []]
    for every, pieces in zip((early, unpack_chunk(swaps[1], plan[1], place)), plan):
        for (which, _, _), cotangent in zip(pieces, every):
            cotangents[which].append(cotangent)
    updated = [None] * 3
    moments = [None] * 3
    passes = []
    for group in ((2,), (0, 1)):
        power, made = adam_pass(
            x_pieces, [cotangents[which] for which in group], [held[which] for which in group]
        )
        passes.append((group, straight_from_others(power, "col"), made))
    for group, powers, made in passes:
        parts = [array for done in made for array in done[:2]]
        after = [array for array in updated if array is not None]
        finished = finish_rows(parts, powers, whole_width, after)
        for which, done, array in zip(group, made, finished):
            updated[which] = array
            moments[which] = done[2:]
    return (*updated, *(done[0] for done in moments), *(done[1] for done in moments))


def solution(mesh):
    tokens_split = P("dp", None)
    split = P("dp", "col")
    return jax.shard_map(
        per_device,
        mesh=mesh,
        in_specs=(split, *(tokens_split,) * 3, *(split,) * 9),
        out_specs=(split,) * 9,
        check_vma=False,
    )
```
